32 devices in a mesh: grp: 4 (over z), slab: 8 (over y, x, core).
Axes of the slice: x: 2, y: 2, z: 4, core: 2. Of those that a mesh axis runs over, the one named last changes fastest.
Arguments:
- snapshots: bfloat16 [4, 128, 32, 8, 128], P('grp', None, 'slab'), may hold values from -24 to 24
- base_flow: float32 [32, 8, 128], P('slab'), may hold values from 0.1 to 0.6
Outputs:
- direct_modes: bfloat16 [128, 32, 8, 128], P('grp', 'slab')
- adjoint_modes: bfloat16 [128, 32, 8, 128], P('grp', 'slab')
The draws below stay inside these ranges and needn't reach their ends.
All inputs are finite; a program needn't handle non-finite values.
Results may differ from the reference program's by a relative error of at most 0.015.
Values may be sent and summed in bfloat16 or wider, within the bound.
No kernel may reach another device: no remote copies, remote signals or barrier semaphores. Data moves between devices by JAX's collectives and lax.ppermute only.
A program may use at most 64 MiB of HBM per device.

```python
import math
import jax
import jax.numpy as jnp
from jax import lax

NY = 8
NZ = 128
SNAP = 128
SECTIONS = 4
NX = 32
N_GRP = 4


def shard_levels(stream_key, dims, cuts, smallest, top_value):
    def one(axis_at, shards_of):
        heights = jax.random.uniform(jax.random.fold_in(jax.random.fold_in(stream_key, 6), axis_at), (shards_of,), jnp.float32, smallest / len(cuts), top_value / len(cuts))
        return jnp.repeat(jnp.exp(heights), dims[axis_at] // shards_of).reshape((-1,) + (1,) * (len(dims) - axis_at - 1))

    gain = one(*cuts[0])
    for cut in cuts[1:]:
        gain = gain * one(*cut)
    return gain


def noise(key, extent, spread, most, split=(), kind=jnp.bfloat16):
    gain = shard_levels(key, extent, split, -0.22, 0.18) if split else 1.0
    result = jax.random.normal(key, extent, jnp.float32) * spread * gain
    return jnp.minimum(jnp.maximum(result, -most), most).astype(kind)


def setup_inputs(seed: int = 0) -> dict:
    streams_of = jax.random.split(jax.random.key(seed), 3)
    snapshots = noise(streams_of[0], (N_GRP, SNAP, NX, NY, NZ), 4.0, 24.0, ((0, 4), (2, 8)))
    base_flow = jnp.clip(0.1 + 0.5 * jax.random.uniform(streams_of[1], (NX, NY, NZ), jnp.float32) ** shard_levels(streams_of[1], (NX, NY, NZ), ((0, 8),), -0.2, 0.2), 0.1, 0.6)
    return dict(snapshots=snapshots, base_flow=base_flow)


diffuse_x = 0.35
diffuse_side = 0.05
keep_center = 0.1
damping = 0.5

def advance(snapshot_field, plus_coef, minus_coef):
    block_size = math.gcd(SNAP, 16)
    blocks = snapshot_field.reshape((SNAP // block_size, block_size) + snapshot_field.shape[1:])

    def sweep_block(snap_block):
        for section_index in range(SECTIONS):
            center = snap_block.astype(jnp.float32)
            ahead_cells = jnp.roll(center, -1, axis=1)
            behind = jnp.roll(center, 1, axis=1)
            side_sum = jnp.roll(center, 1, axis=2) + jnp.roll(center, -1, axis=2)
            side_sum = side_sum + jnp.roll(center, 1, axis=3) + jnp.roll(center, -1, axis=3)
            updated = keep_center * center + plus_coef * ahead_cells + minus_coef * behind + diffuse_side * side_sum
            snap_block = updated.astype(jnp.bfloat16)
        return snap_block
    return lax.map(sweep_block, blocks).reshape(snapshot_field.shape)

def reference(snapshots, base_flow):
    plus_direct = diffuse_x - 0.5 * base_flow
    minus_direct = diffuse_x + 0.5 * base_flow
    plus_adjoint = diffuse_x + 0.5 * jnp.roll(base_flow, -1, axis=0)
    minus_adjoint = diffuse_x - 0.5 * jnp.roll(base_flow, 1, axis=0)
    adjoint = advance(snapshots[N_GRP - 1], plus_adjoint, minus_adjoint).reshape(SNAP, -1)
    norm_scale = 1.0 / math.sqrt(NX * NY * NZ)
    directs = []
    couplings = []
    gram_matrix = jnp.zeros((SNAP, SNAP), jnp.float32)
    for group_index in range(N_GRP - 1):
        direct = advance(snapshots[group_index], plus_direct, minus_direct).reshape(SNAP, -1)
        coupling = lax.dot_general(adjoint.astype(jnp.float32), direct.astype(jnp.float32), (((1,), (1,)), ((), ())), preferred_element_type=jnp.float32) * norm_scale
        gram_matrix = gram_matrix + jnp.dot(coupling, coupling.T, precision=lax.Precision.HIGHEST)
        directs.append(direct)
        couplings.append(coupling)
    energy = jnp.trace(gram_matrix) / SNAP
    system = gram_matrix / energy + damping * jnp.eye(SNAP, dtype=jnp.float32)
    factor = jnp.linalg.cholesky(system)
    inverse = jax.scipy.linalg.cho_solve((factor, True), jnp.eye(SNAP, dtype=jnp.float32))
    total_modes = jnp.zeros((SNAP, NX * NY * NZ), jnp.float32)
    for group_index in range(N_GRP - 1):
        weights = (jnp.dot(inverse, couplings[group_index], precision=lax.Precision.HIGHEST) / jnp.sqrt(energy)).astype(jnp.bfloat16)
        mode_term = jnp.dot(weights.astype(jnp.float32), directs[group_index].astype(jnp.float32), preferred_element_type=jnp.float32)
        total_modes = total_modes + lax.optimization_barrier(mode_term.astype(jnp.bfloat16)).astype(jnp.float32)
    direct_modes = total_modes.astype(jnp.bfloat16).reshape(SNAP, NX, NY, NZ)
    adjoint_modes = jnp.dot(inverse.astype(jnp.bfloat16).astype(jnp.float32), adjoint.astype(jnp.float32), preferred_element_type=jnp.float32)
    adjoint_modes = adjoint_modes.astype(jnp.bfloat16).reshape(SNAP, NX, NY, NZ)
    return (direct_modes, adjoint_modes)
```

```python
import functools
import math

import jax
import jax.numpy as jnp
from jax import lax
from jax.experimental import pallas as pl
from jax.experimental.pallas import tpu as pltpu
from jax.sharding import PartitionSpec as P

SECTIONS = 4
CHUNKS = 1

diffuse_x = 0.35
diffuse_side = 0.05
damping = 0.5

VMEM_LIMIT = 48 * 1024 * 1024
vmem = pl.BlockSpec(memory_space=pltpu.VMEM)
smem = pl.BlockSpec(memory_space=pltpu.SMEM)
anywhere = pl.BlockSpec(memory_space=pl.ANY)
f32 = jnp.float32
bf16 = jnp.bfloat16


def peer(index, step):
    return index ^ step


def swap(value, axis, step):
    count = lax.axis_size(axis)
    return lax.ppermute(value, axis, [(i, i ^ step) for i in range(count)])


def shift(value, axis, step):
    count = lax.axis_size(axis)
    return lax.ppermute(value, axis, [(i, (i + step) % count) for i in range(count)])


def sections_kernel(groups, rows, where_ref, flow_ref, flow_lo, flow_hi, ring_ref,
                    own_ref, lo_ref, hi_ref, *rest):
    outs = rest[:groups]
    flow_ext, plus, minus, stage, first, second = rest[groups:]
    snaps, _, ny, nz = own_ref.shape
    reach = SECTIONS
    me = where_ref[0]
    adj = (me == groups - 1).astype(jnp.int32)
    sign = jnp.where(me == groups - 1, f32(0.5), f32(-0.5))
    flow_ext[0:reach] = flow_lo[...]
    flow_ext[reach:reach + rows] = flow_ref[...]
    flow_ext[reach + rows:] = flow_hi[...]
    total = rows + 2 * reach
    for e in range(1, total - 1):
        plus[e] = diffuse_x + sign * flow_ext[e + adj]
        minus[e] = diffuse_x - sign * flow_ext[e - adj]

    def turn(source, base, count):
        def body(r, carry):
            block = source[:, pl.ds(r, 1)]
            stage[...] = block.astype(f32).reshape(snaps * ny, nz)
            for y in range(ny):
                first[base + r, y] = stage[pl.ds(y, snaps, stride=ny), :].astype(bf16)
            return carry
        lax.fori_loop(0, count, body, 0)

    turn(lo_ref, 0, reach)
    turn(own_ref, reach, rows)
    turn(hi_ref, reach + rows, reach)
    ring = ring_ref[...]

    def one(src, e, y):
        side = jnp.dot(src[e, y], ring, preferred_element_type=f32)
        side = side + src[e, (y + 1) % ny].astype(f32) + src[e, (y - 1) % ny].astype(f32)
        updated = diffuse_side * side
        updated = updated + plus[e][y:y + 1] * src[e + 1, y].astype(f32)
        updated = updated + minus[e][y:y + 1] * src[e - 1, y].astype(f32)
        return updated.astype(bf16)

    bufs = (first, second)
    for s in range(1, SECTIONS):
        src, dst = bufs[(s - 1) % 2], bufs[s % 2]

        def body(e, carry, src=src, dst=dst):
            for y in range(ny):
                dst[e, y] = one(src, e, y)
            return carry
        lax.fori_loop(s, total - s, body, 0)
    src = bufs[(SECTIONS - 1) % 2]
    share = rows // groups
    for k in range(groups):
        for j in range(share):
            e = reach + peer(me, k) * share + j
            for y in range(ny):
                outs[k][j * ny + y] = one(src, e, y)


def sections(where, flow, flow_lo, flow_hi, ring, own, lo, hi, groups):
    snaps, rows, ny, nz = own.shape
    share = rows // groups
    total = rows + 2 * SECTIONS
    return pl.pallas_call(
        functools.partial(sections_kernel, groups, rows),
        out_shape=[jax.ShapeDtypeStruct((share * ny, snaps, nz), bf16)] * groups,
        in_specs=[smem] + [vmem] * 7,
        out_specs=[vmem] * groups,
        scratch_shapes=[
            pltpu.VMEM((total, ny, nz), f32),
            pltpu.VMEM((total, ny, nz), f32),
            pltpu.VMEM((total, ny, nz), f32),
            pltpu.VMEM((snaps * ny, nz), f32),
            pltpu.VMEM((total, ny, snaps, nz), bf16),
            pltpu.VMEM((total, ny, snaps, nz), bf16),
        ],
        compiler_params=pltpu.CompilerParams(vmem_limit_bytes=VMEM_LIMIT),
        name="sections",
    )(where, flow, flow_lo, flow_hi, ring, own, lo, hi)


def coupling_kernel(groups, chunks, where_ref, *rest):
    blocks = rest[: groups * chunks]
    fields, keep, send, scratch, sem = rest[groups * chunks:]
    me, half = where_ref[0], where_ref[1]
    step = blocks[0].shape[1]
    copies = []
    for k in range(groups):
        for c in range(chunks):
            copies.append(pltpu.make_async_copy(
                blocks[k * chunks + c],
                fields.at[peer(me, k), :, pl.ds(c * step, step)],
                sem.at[k * chunks + c]))
    for copy in copies:
        copy.start()
    for copy in copies:
        copy.wait()
    parts, snaps = fields.shape[1], fields.shape[2]
    width = 2 if parts % 2 == 0 else 1

    def wide(g, y):
        return jnp.concatenate([fields[g, y + i] for i in range(width)], axis=1)

    for g in range(groups - 1):
        acc = None
        for y in range(0, parts, width):
            term = lax.dot_general(wide(groups - 1, y), wide(g, y), (((1,), (1,)), ((), ())),
                                   preferred_element_type=f32)
            acc = term if acc is None else acc + term
        scratch[:, g * snaps:(g + 1) * snaps] = acc
    mid = snaps // 2
    keep[...] = scratch[pl.ds(pl.multiple_of(half * mid, mid), mid), :]
    send[...] = scratch[pl.ds(pl.multiple_of((1 - half) * mid, mid), mid), :].astype(send.dtype)


def coupling(where, blocks, groups, chunks):
    parts, step, nz = blocks[0].shape
    snaps = step * chunks
    wide = (groups - 1) * snaps
    return pl.pallas_call(
        functools.partial(coupling_kernel, groups, chunks),
        out_shape=[
            jax.ShapeDtypeStruct((groups, parts, snaps, nz), bf16),
            jax.ShapeDtypeStruct((snaps // 2, wide), f32),
            jax.ShapeDtypeStruct((snaps // 2, wide), f32),
        ],
        in_specs=[smem] + [anywhere] * (groups * chunks),
        out_specs=[vmem] * 3,
        scratch_shapes=[pltpu.VMEM((snaps, wide), f32),
                        pltpu.SemaphoreType.DMA((groups * chunks,))],
        compiler_params=pltpu.CompilerParams(vmem_limit_bytes=VMEM_LIMIT),
        name="coupling",
    )(where, *blocks)


def invert(system):
    size = system.shape[0]
    panels = [system[8 * i:8 * i + 8] for i in range(size // 8)]
    lane = lax.broadcasted_iota(jnp.int32, (8, size), 1)
    row = lax.broadcasted_iota(jnp.int32, (8, size), 0)

    def spread_lane(panel, j):
        return jnp.broadcast_to(panel[:, j:j + 1], (8, size))

    def spread_row(value, j):
        return jnp.broadcast_to(value[j:j + 1], (8, size))

    def small_inverse(a, b, d):
        det = 1.0 / (a * d - b * b)
        return d * det, -b * det, a * det

    for p in range(size // 8):
        for h in range(2):
            base = 8 * p + 4 * h
            lead = panels[p]
            cols = [spread_lane(lead, base + j) for j in range(4)]
            m = [[spread_row(cols[j], 4 * h + i) for j in range(4)] for i in range(4)]
            a0, a1, a2 = small_inverse(m[0][0], m[0][1], m[1][1])
            b00, b01, b10, b11 = m[0][2], m[0][3], m[1][2], m[1][3]
            x00, x01 = a0 * b00 + a1 * b10, a0 * b01 + a1 * b11
            x10, x11 = a1 * b00 + a2 * b10, a1 * b01 + a2 * b11
            s0 = m[2][2] - (b00 * x00 + b10 * x10)
            s1 = m[2][3] - (b00 * x01 + b10 * x11)
            s2 = m[3][3] - (b01 * x01 + b11 * x11)
            d0, d1, d2 = small_inverse(s0, s1, s2)
            y00, y01 = x00 * d0 + x01 * d1, x00 * d1 + x01 * d2
            y10, y11 = x10 * d0 + x11 * d1, x10 * d1 + x11 * d2
            inv = [
                [a0 + y00 * x00 + y01 * x01, a1 + y00 * x10 + y01 * x11, -y00, -y01],
                [None, a2 + y10 * x10 + y11 * x11, -y10, -y11],
                [None, None, d0, d1],
                [None, None, None, d2],
            ]
            for i in range(4):
                for j in range(i):
                    inv[i][j] = inv[j][i]
            rows4 = [spread_row(lead, 4 * h + i) for i in range(4)]
            for i in range(4):
                for j in range(4):
                    rows4[i] = jnp.where(lane == base + j, f32(1.0 if i == j else 0.0), rows4[i])
            new = [sum(inv[i][j] * rows4[j] for j in range(4)) for i in range(4)]
            block = (lane >= base) & (lane < base + 4)
            for q in range(size // 8):
                target = panels[q]
                kept = jnp.where(block, f32(0.0), target)
                if q == p:
                    factors = cols
                else:
                    factors = [spread_lane(target, base + j) for j in range(4)]
                out = kept - sum(factors[j] * new[j] for j in range(4))
                if q == p:
                    for i in range(4):
                        out = jnp.where(row == 4 * h + i, new[i], out)
                panels[q] = out
    return jnp.concatenate(panels, axis=0)


def modes_kernel(groups, where_ref, mine_ref, other_ref, fields, *rest):
    outs = rest[:groups]
    coupling_ref, stage = rest[groups:]
    me, half = where_ref[0], where_ref[1]
    mid = mine_ref.shape[0]
    snaps = 2 * mid
    parts = fields.shape[1]
    scale = where_ref.shape[0]
    coupling_ref[pl.ds(pl.multiple_of(half * mid, mid), mid), :] = mine_ref[...]
    coupling_ref[pl.ds(pl.multiple_of((1 - half) * mid, mid), mid), :] = other_ref[...]
    coupled = coupling_ref[...]
    gram = lax.dot_general(coupled, coupled, (((1,), (1,)), ((), ())),
                           precision=lax.Precision.HIGHEST, preferred_element_type=f32)
    r = lax.broadcasted_iota(jnp.int32, (snaps, snaps), 0)
    c = lax.broadcasted_iota(jnp.int32, (snaps, snaps), 1)
    diagonal = jnp.where(r == c, gram, 0.0)
    energy = jnp.sum(jnp.sum(diagonal, axis=0, keepdims=True), axis=1, keepdims=True) / snaps
    system = gram / energy + jnp.where(r == c, f32(damping), f32(0.0))
    inverse = invert(system)
    weights = jnp.dot(inverse, coupled, precision=lax.Precision.HIGHEST,
                      preferred_element_type=f32) / jnp.sqrt(energy)
    weights = weights.astype(bf16)
    inverse = inverse.astype(bf16)
    share = snaps // groups
    ny = outs[0].shape[3]
    layers = parts // ny
    for which in range(2):
        for layer in range(layers):
            for y in range(ny):
                at = layer * ny + y
                if which == 0:
                    stacked = jnp.concatenate([fields[g, at] for g in range(groups - 1)], axis=0)
                    value = jnp.dot(weights, stacked, preferred_element_type=f32)
                else:
                    value = jnp.dot(inverse, fields[groups - 1, at], preferred_element_type=f32)
                stage[which, layer, pl.ds(y, snaps, stride=ny), :] = value
    for k in range(groups):
        start = pl.multiple_of(peer(me, k) * (share * ny), share * ny)
        for which in range(2):
            for layer in range(layers):
                value = stage[which, layer, pl.ds(start, share * ny), :]
                outs[k][which, :, layer] = value.reshape(share, ny, value.shape[1]).astype(bf16)


def modes(where, mine, other, fields, groups, ny):
    _, parts, snaps, nz = fields.shape
    layers = parts // ny
    share = snaps // groups
    return pl.pallas_call(
        functools.partial(modes_kernel, groups),
        out_shape=[jax.ShapeDtypeStruct((2, share, layers, ny, nz), bf16)] * groups,
        in_specs=[smem, vmem, vmem, vmem],
        out_specs=[vmem] * groups,
        scratch_shapes=[pltpu.VMEM((snaps, mine.shape[1]), f32),
                        pltpu.VMEM((2, layers, snaps * ny, nz), f32)],
        compiler_params=pltpu.CompilerParams(vmem_limit_bytes=VMEM_LIMIT),
        name="modes",
    )(where, mine, other, fields)


def place_kernel(groups, where_ref, *rest):
    blocks = rest[:groups]
    direct, adjoint, sem = rest[groups:]
    me = where_ref[0]
    layers = blocks[0].shape[2]
    copies = []
    for k in range(groups):
        for which, out in enumerate((direct, adjoint)):
            copies.append(pltpu.make_async_copy(
                blocks[k].at[which],
                out.at[:, pl.ds(peer(me, k) * layers, layers)],
                sem.at[2 * k + which]))
    for copy in copies:
        copy.start()
    for copy in copies:
        copy.wait()


def place(where, blocks, groups):
    _, share, layers, ny, nz = blocks[0].shape
    out = jax.ShapeDtypeStruct((share, layers * groups, ny, nz), bf16)
    return pl.pallas_call(
        functools.partial(place_kernel, groups),
        out_shape=[out, out],
        in_specs=[smem] + [anywhere] * groups,
        out_specs=[anywhere] * 2,
        scratch_shapes=[pltpu.SemaphoreType.DMA((2 * groups,))],
        name="place",
    )(where, *blocks)


def per_device(snapshots, base_flow):
    field = snapshots[0]
    snaps, rows, ny, nz = field.shape
    groups = lax.axis_size("grp")
    slabs = lax.axis_size("slab")
    me = lax.axis_index("grp")
    half = lax.axis_index("slab") % 2
    where = jnp.stack([me, half]).astype(jnp.int32)
    flow_lo = shift(base_flow[rows - SECTIONS:], "slab", 1)
    flow_hi = shift(base_flow[:SECTIONS], "slab", -1)
    at = jnp.arange(nz)
    gap = (at[:, None] - at[None, :]) % nz
    ring = (2 * (gap == 0) + (gap == 1) + (gap == nz - 1)).astype(bf16)
    step = snaps // CHUNKS
    blocks = [[None] * CHUNKS for _ in range(groups)]
    for c in range(CHUNKS):
        own = field[c * step:(c + 1) * step]
        lo = shift(own[:, rows - SECTIONS:], "slab", 1)
        hi = shift(own[:, :SECTIONS], "slab", -1)
        parts = sections(where, base_flow, flow_lo, flow_hi, ring, own, lo, hi, groups)
        blocks[0][c] = parts[0]
        for k in range(1, groups):
            blocks[k][c] = swap(parts[k], "grp", k)
    flat = [blocks[k][c] for k in range(groups) for c in range(CHUNKS)]
    fields, keep, send = coupling(where, flat, groups, CHUNKS)
    total = keep + swap(send, "slab", 1)
    bit = 2
    while bit < slabs:
        steps = [bit]
        if 2 * bit < slabs:
            steps += [2 * bit, 3 * bit]
        sent = total.astype(bf16)
        total = sum((swap(sent, "slab", s).astype(f32) for s in steps), total)
        bit *= 4
    sent = total.astype(bf16)
    total = sum((swap(sent, "grp", s).astype(f32) for s in range(1, groups)), total)
    mine = total * (1.0 / math.sqrt(rows * slabs * ny * nz))
    other = swap(mine, "slab", 1)
    outs = modes(where, mine, other, fields, groups, ny)
    outs = [outs[0]] + [swap(outs[k], "grp", k) for k in range(1, groups)]
    return tuple(place(where, outs, groups))


def solution(mesh):
    return jax.shard_map(
        per_device,
        mesh=mesh,
        in_specs=(P("grp", None, "slab", None, None), P("slab", None, None)),
        out_specs=(P("grp", "slab", None, None), P("grp", "slab", None, None)),
        check_vma=False,
    )
```

```python
import functools
import math

import jax
import jax.numpy as jnp
from jax import lax
from jax.experimental import pallas as pl
from jax.experimental.pallas import tpu as pltpu
from jax.sharding import PartitionSpec as P

SECTIONS = 4
CHUNKS = (1, 1)
ORDER = (1, 2, 3)
UNROLL = 2

diffuse_x = 0.35
diffuse_side = 0.05
damping = 0.5

VMEM_LIMIT = 48 * 1024 * 1024
vmem = pl.BlockSpec(memory_space=pltpu.VMEM)
smem = pl.BlockSpec(memory_space=pltpu.SMEM)
anywhere = pl.BlockSpec(memory_space=pl.ANY)
hbm = pl.BlockSpec(memory_space=pltpu.HBM)
f32 = jnp.float32
bf16 = jnp.bfloat16


def peer(index, step):
    return index ^ step


def swap(value, axis, step):
    count = lax.axis_size(axis)
    return lax.ppermute(value, axis, [(i, i ^ step) for i in range(count)])


def shift(value, axis, step):
    count = lax.axis_size(axis)
    return lax.ppermute(value, axis, [(i, (i + step) % count) for i in range(count)])


def pack_kernel(start, with_flow, flow_ref, field_ref, out, block, stage, sem):
    step, rows, ny, nz = block.shape
    copy = pltpu.make_async_copy(field_ref.at[pl.ds(start, step)], block, sem)
    copy.start()
    if with_flow:
        per = step // (rows * ny)
        left = flow_ref[...].reshape(rows * ny, nz)
        for p in range(3):
            part = left.astype(bf16)
            left = left - part.astype(f32)
            at = p % per * rows * ny
            out[rows * ny + p // per, at:at + rows * ny] = part
    copy.wait()
    for r in range(rows):
        stage[r % 2] = block[:, r].astype(f32).reshape(step * ny, nz)
        for y in range(ny):
            out[r * ny + y] = stage[r % 2, pl.ds(y, step, stride=ny), :].astype(bf16)


def pack(flow, field, start, step, with_flow):
    _, rows, ny, nz = field.shape
    extra = -(-3 // (step // (rows * ny))) if with_flow else 0
    return pl.pallas_call(
        functools.partial(pack_kernel, start, with_flow),
        out_shape=jax.ShapeDtypeStruct((rows * ny + extra, step, nz), bf16),
        in_specs=[vmem, hbm],
        out_specs=vmem,
        scratch_shapes=[
            pltpu.VMEM((step, rows, ny, nz), bf16),
            pltpu.VMEM((2, step * ny, nz), f32),
            pltpu.SemaphoreType.DMA(()),
        ],
        compiler_params=pltpu.CompilerParams(vmem_limit_bytes=VMEM_LIMIT),
        name="pack",
    )(flow, field)


def sections_kernel(groups, rows, ny, lead, where_ref, ring_ref, *rest):
    reach = SECTIONS
    total = rows + 2 * reach
    me = where_ref[0]
    if lead:
        flow_ref, own_ref, lo_ref, hi_ref = rest[:4]
        outs = rest[4:4 + groups]
        plus, minus, flow_ext, first, second = rest[4 + groups:]
    else:
        plus, minus, own_ref, lo_ref, hi_ref, _ = rest[:6]
        outs = rest[6:6 + groups]
        first, second = rest[6 + groups:]
    step, nz = own_ref.shape[1:]
    if lead:
        adj = (me == groups - 1).astype(jnp.int32)
        sign = jnp.where(me == groups - 1, f32(0.5), f32(-0.5))
        per = step // (rows * ny)

        def flow_of(ref):
            flow = None
            for p in (2, 1, 0):
                at = p % per * rows * ny
                part = ref[rows * ny + p // per, at:at + rows * ny].astype(f32)
                flow = part if flow is None else flow + part
            return flow.reshape(rows, ny, nz)

        flow_ext[0:reach] = flow_of(lo_ref)[rows - reach:]
        flow_ext[reach:reach + rows] = flow_ref[...]
        flow_ext[reach + rows:] = flow_of(hi_ref)[:reach]
        for e in range(1, total - 1):
            plus[e] = diffuse_x + sign * flow_ext[e + adj]
            minus[e] = diffuse_x - sign * flow_ext[e - adj]
    ring = ring_ref[...]

    def entry(e, y):
        if e < reach:
            return lo_ref[(rows - reach + e) * ny + y]
        if e < reach + rows:
            return own_ref[(e - reach) * ny + y]
        return hi_ref[(e - reach - rows) * ny + y]

    def one(src, e, y):
        get = entry if src is None else lambda at, w: src[at, w]
        side = jnp.dot(get(e, y), ring, preferred_element_type=f32)
        side = side + get(e, (y + 1) % ny).astype(f32) + get(e, (y - 1) % ny).astype(f32)
        updated = diffuse_side * side
        updated = updated + plus[e, y:y + 1, :] * get(e + 1, y).astype(f32)
        updated = updated + minus[e, y:y + 1, :] * get(e - 1, y).astype(f32)
        return updated.astype(bf16)

    for e in range(1, total - 1):
        for y in range(ny):
            first[e, y] = one(None, e, y)
    bufs = (first, second)
    for s in range(2, SECTIONS):
        src, dst = bufs[s % 2], bufs[(s - 1) % 2]

        def body(e, carry, src=src, dst=dst):
            for y in range(ny):
                dst[e, y] = one(src, e, y)
            return carry
        lax.fori_loop(s, total - s, body, 0, unroll=UNROLL)
    src = bufs[SECTIONS % 2]
    share = rows // groups
    for k in range(groups):
        for j in range(share):
            e = reach + peer(me, k) * share + j
            for y in range(ny):
                outs[k][j * ny + y] = one(src, e, y)


def sections(where, ring, coefs, own, lo, hi, groups, flow, before):
    rows, ny, nz = flow.shape
    step = own.shape[1]
    share = rows // groups
    total = rows + 2 * SECTIONS
    lead = coefs is None
    out = [jax.ShapeDtypeStruct((share * ny, step, nz), bf16)] * groups
    scratch = [pltpu.VMEM((total, ny, step, nz), bf16)] * 2
    if lead:
        out += [jax.ShapeDtypeStruct((total, ny, nz), f32)] * 2
        scratch = [pltpu.VMEM((total, ny, nz), f32)] + scratch
        coefs = [flow]
    outs = pl.pallas_call(
        functools.partial(sections_kernel, groups, rows, ny, lead),
        out_shape=out,
        in_specs=[smem] + [vmem] * (4 + len(coefs)) + [anywhere] * len(before),
        out_specs=[vmem] * len(out),
        scratch_shapes=scratch,
        compiler_params=pltpu.CompilerParams(vmem_limit_bytes=VMEM_LIMIT),
        cost_estimate=pl.CostEstimate(
            flops=8 * SECTIONS * step * total * ny * nz, bytes_accessed=8 * step * rows * ny * nz, transcendentals=0),
        name="sections",
    )(where, ring, *coefs, own, lo, hi, *before)
    return outs[:groups], outs[groups:]


def coupling_kernel(groups, chunks, where_ref, *rest):
    blocks = rest[: groups * chunks]
    fields, keep, send, scratch, sem = rest[groups * chunks:]
    me, half = where_ref[0], where_ref[1]
    copies = []
    for k in range(groups):
        start = 0
        for c in range(chunks):
            step = blocks[c].shape[1]
            copies.append(pltpu.make_async_copy(
                blocks[k * chunks + c],
                fields.at[peer(me, k), :, pl.ds(start, step)],
                sem.at[k * chunks + c]))
            start += step
    for copy in copies:
        copy.start()
    for copy in copies:
        copy.wait()
    parts, snaps = fields.shape[1], fields.shape[2]
    width = 2 if parts % 2 == 0 else 1

    def wide(g, y):
        return jnp.concatenate([fields[g, y + i] for i in range(width)], axis=1)

    for g in range(groups - 1):
        acc = None
        for y in range(0, parts, width):
            term = lax.dot_general(wide(groups - 1, y), wide(g, y), (((1,), (1,)), ((), ())),
                                   preferred_element_type=f32)
            acc = term if acc is None else acc + term
        scratch[:, g * snaps:(g + 1) * snaps] = acc
    mid = snaps // 2
    keep[...] = scratch[pl.ds(pl.multiple_of(half * mid, mid), mid), :]
    send[...] = scratch[pl.ds(pl.multiple_of((1 - half) * mid, mid), mid), :].astype(send.dtype)


def coupling(where, blocks, groups, chunks):
    parts, _, nz = blocks[0].shape
    snaps = sum(block.shape[1] for block in blocks[:chunks])
    wide = (groups - 1) * snaps
    return pl.pallas_call(
        functools.partial(coupling_kernel, groups, chunks),
        out_shape=[
            jax.ShapeDtypeStruct((groups, parts, snaps, nz), bf16),
            jax.ShapeDtypeStruct((snaps // 2, wide), f32),
            jax.ShapeDtypeStruct((snaps // 2, wide), f32),
        ],
        in_specs=[smem] + [anywhere] * (groups * chunks),
        out_specs=[vmem] * 3,
        scratch_shapes=[pltpu.VMEM((snaps, wide), f32),
                        pltpu.SemaphoreType.DMA((groups * chunks,))],
        compiler_params=pltpu.CompilerParams(vmem_limit_bytes=VMEM_LIMIT),
        name="coupling",
    )(where, *blocks)


def invert(system):
    size = system.shape[0]
    panels = [system[8 * i:8 * i + 8] for i in range(size // 8)]
    lane = lax.broadcasted_iota(jnp.int32, (8, size), 1)
    row = lax.broadcasted_iota(jnp.int32, (8, size), 0)

    def spread_lane(panel, j):
        return jnp.broadcast_to(panel[:, j:j + 1], (8, size))

    def spread_row(value, j):
        return jnp.broadcast_to(value[j:j + 1], (8, size))

    def small_inverse(a, b, d):
        det = 1.0 / (a * d - b * b)
        return d * det, -b * det, a * det

    for p in range(size // 8):
        for h in range(2):
            base = 8 * p + 4 * h
            lead = panels[p]
            cols = [spread_lane(lead, base + j) for j in range(4)]
            m = [[spread_row(cols[j], 4 * h + i) for j in range(4)] for i in range(4)]
            a0, a1, a2 = small_inverse(m[0][0], m[0][1], m[1][1])
            b00, b01, b10, b11 = m[0][2], m[0][3], m[1][2], m[1][3]
            x00, x01 = a0 * b00 + a1 * b10, a0 * b01 + a1 * b11
            x10, x11 = a1 * b00 + a2 * b10, a1 * b01 + a2 * b11
            s0 = m[2][2] - (b00 * x00 + b10 * x10)
            s1 = m[2][3] - (b00 * x01 + b10 * x11)
            s2 = m[3][3] - (b01 * x01 + b11 * x11)
            d0, d1, d2 = small_inverse(s0, s1, s2)
            y00, y01 = x00 * d0 + x01 * d1, x00 * d1 + x01 * d2
            y10, y11 = x10 * d0 + x11 * d1, x10 * d1 + x11 * d2
            inv = [
                [a0 + y00 * x00 + y01 * x01, a1 + y00 * x10 + y01 * x11, -y00, -y01],
                [None, a2 + y10 * x10 + y11 * x11, -y10, -y11],
                [None, None, d0, d1],
                [None, None, None, d2],
            ]
            for i in range(4):
                for j in range(i):
                    inv[i][j] = inv[j][i]
            rows4 = [spread_row(lead, 4 * h + i) for i in range(4)]
            for i in range(4):
                for j in range(4):
                    rows4[i] = jnp.where(lane == base + j, f32(1.0 if i == j else 0.0), rows4[i])
            new = [sum(inv[i][j] * rows4[j] for j in range(4)) for i in range(4)]
            block = (lane >= base) & (lane < base + 4)
            for q in range(size // 8):
                target = panels[q]
                kept = jnp.where(block, f32(0.0), target)
                if q == p:
                    factors = cols
                else:
                    factors = [spread_lane(target, base + j) for j in range(4)]
                out = kept - sum(factors[j] * new[j] for j in range(4))
                if q == p:
                    for i in range(4):
                        out = jnp.where(row == 4 * h + i, new[i], out)
                panels[q] = out
    return jnp.concatenate(panels, axis=0)


def modes_kernel(groups, where_ref, mine_ref, other_ref, fields, *rest):
    outs = rest[:groups]
    coupling_ref, stage = rest[groups:]
    me, half = where_ref[0], where_ref[1]
    mid = mine_ref.shape[0]
    snaps = 2 * mid
    parts = fields.shape[1]
    scale = where_ref.shape[0]
    coupling_ref[pl.ds(pl.multiple_of(half * mid, mid), mid), :] = mine_ref[...]
    coupling_ref[pl.ds(pl.multiple_of((1 - half) * mid, mid), mid), :] = other_ref[...]
    coupled = coupling_ref[...]
    gram = lax.dot_general(coupled, coupled, (((1,), (1,)), ((), ())),
                           precision=lax.Precision.HIGHEST, preferred_element_type=f32)
    r = lax.broadcasted_iota(jnp.int32, (snaps, snaps), 0)
    c = lax.broadcasted_iota(jnp.int32, (snaps, snaps), 1)
    diagonal = jnp.where(r == c, gram, 0.0)
    energy = jnp.sum(jnp.sum(diagonal, axis=0, keepdims=True), axis=1, keepdims=True) / snaps
    system = gram / energy + jnp.where(r == c, f32(damping), f32(0.0))
    inverse = invert(system)
    weights = jnp.dot(inverse, coupled, precision=lax.Precision.HIGHEST,
                      preferred_element_type=f32) / jnp.sqrt(energy)
    weights = weights.astype(bf16)
    inverse = inverse.astype(bf16)
    share = snaps // groups
    ny = outs[0].shape[3]
    layers = parts // ny
    for which in range(2):
        for layer in range(layers):
            for y in range(ny):
                at = layer * ny + y
                if which == 0:
                    stacked = jnp.concatenate([fields[g, at] for g in range(groups - 1)], axis=0)
                    value = jnp.dot(weights, stacked, preferred_element_type=f32)
                else:
                    value = jnp.dot(inverse, fields[groups - 1, at], preferred_element_type=f32)
                stage[which, layer, pl.ds(y, snaps, stride=ny), :] = value
    for k in range(groups):
        start = pl.multiple_of(peer(me, k) * (share * ny), share * ny)
        for which in range(2):
            for layer in range(layers):
                value = stage[which, layer, pl.ds(start, share * ny), :]
                outs[k][which, :, layer] = value.reshape(share, ny, value.shape[1]).astype(bf16)


def modes(where, mine, other, fields, groups, ny):
    _, parts, snaps, nz = fields.shape
    layers = parts // ny
    share = snaps // groups
    return pl.pallas_call(
        functools.partial(modes_kernel, groups),
        out_shape=[jax.ShapeDtypeStruct((2, share, layers, ny, nz), bf16)] * groups,
        in_specs=[smem, vmem, vmem, vmem],
        out_specs=[vmem] * groups,
        scratch_shapes=[pltpu.VMEM((snaps, mine.shape[1]), f32),
                        pltpu.VMEM((2, layers, snaps * ny, nz), f32)],
        compiler_params=pltpu.CompilerParams(vmem_limit_bytes=VMEM_LIMIT),
        name="modes",
    )(where, mine, other, fields)


def place_kernel(groups, where_ref, *rest):
    blocks = rest[:groups]
    outs = rest[groups:]
    me = where_ref[0]
    layers = blocks[0].shape[2]
    for k in range(groups):
        for which in range(2):
            for layer in range(layers):
                outs[which][:, peer(me, k) * layers + layer] = blocks[k][which, :, layer]


def place(where, blocks, groups):
    _, share, layers, ny, nz = blocks[0].shape
    out = jax.ShapeDtypeStruct((share, layers * groups, ny, nz), bf16)
    return pl.pallas_call(
        functools.partial(place_kernel, groups),
        out_shape=[out, out],
        in_specs=[smem] + [vmem] * groups,
        out_specs=[vmem] * 2,
        name="place",
    )(where, *blocks)


def per_device(snapshots, base_flow):
    field = snapshots[0]
    snaps, rows, ny, nz = field.shape
    groups = lax.axis_size("grp")
    slabs = lax.axis_size("slab")
    me = lax.axis_index("grp")
    half = lax.axis_index("slab") % 2
    where = jnp.stack([me, half]).astype(jnp.int32)
    at = jnp.arange(nz)
    gap = (at[:, None] - at[None, :]) % nz
    ring = (2 * (gap == 0) + (gap == 1) + (gap == nz - 1)).astype(bf16)
    sizes = [snaps * part // sum(CHUNKS) for part in CHUNKS]
    chunks = len(sizes)
    blocks = [[None] * chunks for _ in range(groups)]
    coefs = None
    for c in range(chunks):
        own = pack(base_flow, field, sum(sizes[:c]), sizes[c], c == 0)
        lo = shift(own, "slab", 1)
        hi = shift(own, "slab", -1)
        before = [blocks[ORDER[0]][c - 1]] if c else []
        parts, made = sections(where, ring, coefs, own, lo, hi, groups, base_flow, before)
        coefs = coefs or made
        blocks[0][c] = parts[0]
        for k in ORDER:
            blocks[k][c] = swap(parts[k], "grp", k)
    flat = [blocks[k][c] for k in range(groups) for c in range(chunks)]
    fields, keep, send = coupling(where, flat, groups, chunks)
    total = keep + swap(send, "slab", 1)
    bit = 2
    while bit < slabs:
        steps = [bit]
        if 2 * bit < slabs:
            steps += [2 * bit, 3 * bit]
        sent = total.astype(bf16)
        total = sum((swap(sent, "slab", s).astype(f32) for s in steps), total)
        bit *= 4
    sent = total.astype(bf16)
    total = sum((swap(sent, "grp", s).astype(f32) for s in range(1, groups)), total)
    mine = total * (1.0 / math.sqrt(rows * slabs * ny * nz))
    other = swap(mine, "slab", 1)
    outs = modes(where, mine, other, fields, groups, ny)
    outs = [outs[0]] + [swap(outs[k], "grp", k) for k in range(1, groups)]
    return tuple(place(where, outs, groups))


def solution(mesh):
    return jax.shard_map(
        per_device,
        mesh=mesh,
        in_specs=(P("grp", None, "slab", None, None), P("slab", None, None)),
        out_specs=(P("grp", "slab", None, None), P("grp", "slab", None, None)),
        check_vma=False,
    )
```

```python
import functools
import math

import jax
import jax.numpy as jnp
from jax import lax
from jax.experimental import pallas as pl
from jax.experimental.pallas import tpu as pltpu
from jax.sharding import PartitionSpec as P

SECTIONS = 4
CHUNKS = (1, 1)
UNROLL = 4

diffuse_x = 0.35
diffuse_side = 0.05
damping = 0.5

VMEM_LIMIT = 48 * 1024 * 1024
vmem = pl.BlockSpec(memory_space=pltpu.VMEM)
smem = pl.BlockSpec(memory_space=pltpu.SMEM)
anywhere = pl.BlockSpec(memory_space=pl.ANY)
hbm = pl.BlockSpec(memory_space=pltpu.HBM)
f32 = jnp.float32
bf16 = jnp.bfloat16


def peer(index, step):
    return index ^ step


def swap(value, axis, step):
    count = lax.axis_size(axis)
    return lax.ppermute(value, axis, [(i, i ^ step) for i in range(count)])


def shift(value, axis, step):
    count = lax.axis_size(axis)
    return lax.ppermute(value, axis, [(i, (i + step) % count) for i in range(count)])


def pack_kernel(start, with_flow, flow_ref, field_ref, out, block, stage, sem):
    step, rows, ny, nz = block.shape
    copy = pltpu.make_async_copy(field_ref.at[pl.ds(start, step)], block, sem)
    copy.start()
    if with_flow:
        per = step // (rows * ny)
        left = flow_ref[...].reshape(rows * ny, nz)
        for p in range(3):
            part = left.astype(bf16)
            left = left - part.astype(f32)
            at = p % per * rows * ny
            out[rows * ny + p // per, at:at + rows * ny] = part
    copy.wait()
    for r in range(rows):
        stage[r % 2] = block[:, r].astype(f32).reshape(step * ny, nz)
        for y in range(ny):
            out[r * ny + y] = stage[r % 2, pl.ds(y, step, stride=ny), :].astype(bf16)


def pack(flow, field, start, step, with_flow):
    _, rows, ny, nz = field.shape
    extra = -(-3 // (step // (rows * ny))) if with_flow else 0
    return pl.pallas_call(
        functools.partial(pack_kernel, start, with_flow),
        out_shape=jax.ShapeDtypeStruct((rows * ny + extra, step, nz), bf16),
        in_specs=[vmem, hbm],
        out_specs=vmem,
        scratch_shapes=[
            pltpu.VMEM((step, rows, ny, nz), bf16),
            pltpu.VMEM((2, step * ny, nz), f32),
            pltpu.SemaphoreType.DMA(()),
        ],
        compiler_params=pltpu.CompilerParams(vmem_limit_bytes=VMEM_LIMIT),
        name="pack",
    )(flow, field)


def sections_kernel(groups, rows, ny, lead, where_ref, ring_ref, *rest):
    reach = SECTIONS
    total = rows + 2 * reach
    me = where_ref[0]
    if lead:
        flow_ref, own_ref, lo_ref, hi_ref = rest[:4]
        outs = rest[4:4 + groups]
        plus, minus, flow_ext, first, second = rest[4 + groups:]
    else:
        plus, minus, own_ref, lo_ref, hi_ref, _ = rest[:6]
        outs = rest[6:6 + groups]
        first, second = rest[6 + groups:]
    step, nz = own_ref.shape[1:]
    if lead:
        adj = (me == groups - 1).astype(jnp.int32)
        sign = jnp.where(me == groups - 1, f32(1.0), f32(-1.0))
        per = step // (rows * ny)

        def flow_of(ref):
            flow = None
            for p in (2, 1, 0):
                at = p % per * rows * ny
                part = ref[rows * ny + p // per, at:at + rows * ny].astype(f32)
                flow = part if flow is None else flow + part
            return flow.reshape(rows, ny, nz)

        flow_ext[0:reach] = flow_of(lo_ref)[rows - reach:]
        flow_ext[reach:reach + rows] = flow_ref[...]
        flow_ext[reach + rows:] = flow_of(hi_ref)[:reach]
        for e in range(1, total - 1):
            plus[e] = diffuse_x + sign * flow_ext[e + adj]
            minus[e] = diffuse_x - sign * flow_ext[e - adj]
    ring = ring_ref[...]

    def entry(e, y):
        if e < reach:
            return lo_ref[(rows - reach + e) * ny + y]
        if e < reach + rows:
            return own_ref[(e - reach) * ny + y]
        return hi_ref[(e - reach - rows) * ny + y]

    def one(src, e, y):
        get = entry if src is None else lambda at, w: src[at, w]
        side = jnp.dot(get(e, y), ring, preferred_element_type=f32)
        side = side + get(e, (y + 1) % ny).astype(f32) + get(e, (y - 1) % ny).astype(f32)
        updated = diffuse_side * side
        updated = updated + plus[e, y:y + 1, :] * get(e + 1, y).astype(f32)
        updated = updated + minus[e, y:y + 1, :] * get(e - 1, y).astype(f32)
        return updated.astype(bf16)

    for e in range(1, total - 1):
        for y in range(ny):
            first[e, y] = one(None, e, y)
    bufs = (first, second)
    for s in range(2, SECTIONS):
        src, dst = bufs[s % 2], bufs[(s - 1) % 2]

        def body(e, carry, src=src, dst=dst):
            for y in range(ny):
                dst[e, y] = one(src, e, y)
            return carry
        lax.fori_loop(s, total - s, body, 0, unroll=UNROLL)
    src = bufs[SECTIONS % 2]
    share = rows // groups
    for k in range(groups):
        for j in range(share):
            e = reach + peer(me, k) * share + j
            for y in range(ny):
                outs[k][j * ny + y] = one(src, e, y)


def sections(where, ring, coefs, own, lo, hi, groups, flow, before):
    rows, ny, nz = flow.shape
    step = own.shape[1]
    share = rows // groups
    total = rows + 2 * SECTIONS
    lead = coefs is None
    out = [jax.ShapeDtypeStruct((share * ny, step, nz), bf16)] * groups
    scratch = [pltpu.VMEM((total, ny, step, nz), bf16)] * 2
    if lead:
        out += [jax.ShapeDtypeStruct((total, ny, nz), f32)] * 2
        scratch = [pltpu.VMEM((total, ny, nz), f32)] + scratch
        coefs = [flow]
    outs = pl.pallas_call(
        functools.partial(sections_kernel, groups, rows, ny, lead),
        out_shape=out,
        in_specs=[smem] + [vmem] * (4 + len(coefs)) + [anywhere] * len(before),
        out_specs=[vmem] * len(out),
        scratch_shapes=scratch,
        compiler_params=pltpu.CompilerParams(vmem_limit_bytes=VMEM_LIMIT),
        cost_estimate=pl.CostEstimate(
            flops=8 * SECTIONS * step * total * ny * nz, bytes_accessed=8 * step * rows * ny * nz, transcendentals=0),
        name="sections",
    )(where, ring, *coefs, own, lo, hi, *before)
    return outs[:groups], outs[groups:]


def by_group(me, groups, action):
    for g in range(groups):
        pl.when(me == g)(functools.partial(action, g))


def coupling_kernel(groups, chunks, where_ref, *rest):
    blocks = rest[: groups * chunks]
    keep, send, scratch = rest[groups * chunks:]
    me, half = where_ref[0], where_ref[1]
    parts = blocks[0].shape[0]
    width = 2 if parts % 2 == 0 else 1
    snaps = scratch.shape[0]

    def action(mine):
        def wide(g, y):
            own = blocks[peer(mine, g) * chunks:(peer(mine, g) + 1) * chunks]
            return jnp.concatenate([
                jnp.concatenate([block[y + i] for block in own], axis=0) for i in range(width)
            ], axis=1)

        total = None
        for y in range(0, parts, width):
            direct = jnp.concatenate([wide(g, y) for g in range(groups - 1)], axis=0)
            term = lax.dot_general(wide(groups - 1, y), direct, (((1,), (1,)), ((), ())),
                                   preferred_element_type=f32)
            total = term if total is None else total + term
        scratch[...] = total

    by_group(me, groups, action)
    mid = snaps // 2
    keep[...] = scratch[pl.ds(pl.multiple_of(half * mid, mid), mid), :]
    send[...] = scratch[pl.ds(pl.multiple_of((1 - half) * mid, mid), mid), :]


def coupling(where, blocks, groups, chunks):
    snaps = sum(block.shape[1] for block in blocks[:chunks])
    wide = (groups - 1) * snaps
    return pl.pallas_call(
        functools.partial(coupling_kernel, groups, chunks),
        out_shape=[jax.ShapeDtypeStruct((snaps // 2, wide), f32)] * 2,
        in_specs=[smem] + [vmem] * (groups * chunks),
        out_specs=[vmem] * 2,
        scratch_shapes=[pltpu.VMEM((snaps, wide), f32)],
        compiler_params=pltpu.CompilerParams(vmem_limit_bytes=VMEM_LIMIT),
        name="coupling",
    )(where, *blocks)


def invert(system):
    size = system.shape[0]
    panels = [system[8 * i:8 * i + 8] for i in range(size // 8)]
    lane = lax.broadcasted_iota(jnp.int32, (8, size), 1)
    row = lax.broadcasted_iota(jnp.int32, (8, size), 0)

    def spread_lane(panel, j):
        return jnp.broadcast_to(panel[:, j:j + 1], (8, size))

    def spread_row(value, j):
        return jnp.broadcast_to(value[j:j + 1], (8, size))

    def small_inverse(a, b, d):
        det = a * d - b * b
        guess = pl.reciprocal(det, approx=True)
        guess = guess * (2.0 - det * guess)
        det = guess * (2.0 - det * guess)
        return d * det, -b * det, a * det

    for p in range(size // 8):
        for h in range(2):
            base = 8 * p + 4 * h
            lead = panels[p]
            cols = [spread_lane(lead, base + j) for j in range(4)]
            m = [[spread_row(cols[j], 4 * h + i) for j in range(4)] for i in range(4)]
            a0, a1, a2 = small_inverse(m[0][0], m[0][1], m[1][1])
            b00, b01, b10, b11 = m[0][2], m[0][3], m[1][2], m[1][3]
            x00, x01 = a0 * b00 + a1 * b10, a0 * b01 + a1 * b11
            x10, x11 = a1 * b00 + a2 * b10, a1 * b01 + a2 * b11
            s0 = m[2][2] - (b00 * x00 + b10 * x10)
            s1 = m[2][3] - (b00 * x01 + b10 * x11)
            s2 = m[3][3] - (b01 * x01 + b11 * x11)
            d0, d1, d2 = small_inverse(s0, s1, s2)
            y00, y01 = x00 * d0 + x01 * d1, x00 * d1 + x01 * d2
            y10, y11 = x10 * d0 + x11 * d1, x10 * d1 + x11 * d2
            inv = [
                [a0 + y00 * x00 + y01 * x01, a1 + y00 * x10 + y01 * x11, -y00, -y01],
                [None, a2 + y10 * x10 + y11 * x11, -y10, -y11],
                [None, None, d0, d1],
                [None, None, None, d2],
            ]
            for i in range(4):
                for j in range(i):
                    inv[i][j] = inv[j][i]
            rows4 = [spread_row(lead, 4 * h + i) for i in range(4)]
            for i in range(4):
                for j in range(4):
                    rows4[i] = jnp.where(lane == base + j, f32(1.0 if i == j else 0.0), rows4[i])
            new = [sum(inv[i][j] * rows4[j] for j in range(4)) for i in range(4)]
            block = (lane >= base) & (lane < base + 4)
            for q in range(size // 8):
                target = panels[q]
                kept = jnp.where(block, f32(0.0), target)
                if q == p:
                    factors = cols
                else:
                    factors = [spread_lane(target, base + j) for j in range(4)]
                out = kept - sum(factors[j] * new[j] for j in range(4))
                if q == p:
                    for i in range(4):
                        out = jnp.where(row == 4 * h + i, new[i], out)
                panels[q] = out
    return jnp.concatenate(panels, axis=0)


def modes_kernel(groups, chunks, where_ref, mine_ref, other_ref, *rest):
    blocks = rest[:groups * chunks]
    outs = rest[groups * chunks:groups * (chunks + 1)]
    coupling_ref, stage = rest[groups * (chunks + 1):]
    me, half = where_ref[0], where_ref[1]
    mid = mine_ref.shape[0]
    snaps = 2 * mid
    parts = blocks[0].shape[0]
    coupling_ref[pl.ds(pl.multiple_of(half * mid, mid), mid), :] = mine_ref[...]
    coupling_ref[pl.ds(pl.multiple_of((1 - half) * mid, mid), mid), :] = other_ref[...]
    coupled = coupling_ref[...]
    gram = lax.dot_general(coupled, coupled, (((1,), (1,)), ((), ())),
                           precision=lax.Precision.HIGHEST, preferred_element_type=f32)
    r = lax.broadcasted_iota(jnp.int32, (snaps, snaps), 0)
    c = lax.broadcasted_iota(jnp.int32, (snaps, snaps), 1)
    diagonal = jnp.where(r == c, gram, 0.0)
    energy = jnp.sum(jnp.sum(diagonal, axis=0, keepdims=True), axis=1, keepdims=True) / snaps
    system = gram / energy + jnp.where(r == c, f32(damping), f32(0.0))
    inverse = invert(system)
    weights = jnp.dot(inverse, coupled, precision=lax.Precision.HIGHEST,
                      preferred_element_type=f32) / jnp.sqrt(energy)
    weights = weights.astype(bf16)
    inverse = inverse.astype(bf16)
    share = snaps // groups
    ny = outs[0].shape[3]
    layers = parts // ny

    def action(mine):
        def group(g, at):
            return [block[at] for block in blocks[peer(mine, g) * chunks:(peer(mine, g) + 1) * chunks]]

        for layer in range(layers):
            for y in range(ny):
                at = layer * ny + y
                rows = pl.ds(y, snaps, stride=ny)
                direct = jnp.concatenate(
                    [part for g in range(groups - 1) for part in group(g, at)], axis=0)
                adjoint = jnp.concatenate(group(groups - 1, at), axis=0)
                stage[0, layer, rows, :] = jnp.dot(weights, direct, preferred_element_type=f32)
                stage[1, layer, rows, :] = jnp.dot(inverse, adjoint, preferred_element_type=f32)

    by_group(me, groups, action)
    for k in range(groups):
        start = pl.multiple_of(peer(me, k) * (share * ny), share * ny)
        for which in range(2):
            for layer in range(layers):
                value = stage[which, layer, pl.ds(start, share * ny), :]
                outs[k][which, :, layer] = value.reshape(share, ny, value.shape[1]).astype(bf16)


def modes(where, mine, other, blocks, groups, ny):
    chunks = len(blocks) // groups
    parts, _, nz = blocks[0].shape
    snaps = 2 * mine.shape[0]
    layers = parts // ny
    share = snaps // groups
    return pl.pallas_call(
        functools.partial(modes_kernel, groups, chunks),
        out_shape=[jax.ShapeDtypeStruct((2, share, layers, ny, nz), bf16)] * groups,
        in_specs=[smem, vmem, vmem] + [vmem] * len(blocks),
        out_specs=[vmem] * groups,
        scratch_shapes=[pltpu.VMEM((snaps, mine.shape[1]), f32),
                        pltpu.VMEM((2, layers, snaps * ny, nz), f32)],
        compiler_params=pltpu.CompilerParams(vmem_limit_bytes=VMEM_LIMIT),
        name="modes",
    )(where, mine, other, *blocks)


def place_kernel(groups, where_ref, *rest):
    blocks = rest[:groups]
    outs = rest[groups:]
    me = where_ref[0]
    layers = blocks[0].shape[2]
    for k in range(groups):
        for which in range(2):
            for layer in range(layers):
                outs[which][:, peer(me, k) * layers + layer] = blocks[k][which, :, layer]


def place(where, blocks, groups):
    _, share, layers, ny, nz = blocks[0].shape
    out = jax.ShapeDtypeStruct((share, layers * groups, ny, nz), bf16)
    return pl.pallas_call(
        functools.partial(place_kernel, groups),
        out_shape=[out, out],
        in_specs=[smem] + [vmem] * groups,
        out_specs=[vmem] * 2,
        compiler_params=pltpu.CompilerParams(vmem_limit_bytes=8 * 1024 * 1024),
        name="place",
    )(where, *blocks)


def per_device(snapshots, base_flow):
    field = snapshots[0]
    snaps, rows, ny, nz = field.shape
    groups = lax.axis_size("grp")
    slabs = lax.axis_size("slab")
    me = lax.axis_index("grp")
    half = lax.axis_index("slab") % 2
    where = jnp.stack([me, half]).astype(jnp.int32)
    flow = 0.5 * base_flow
    at = jnp.arange(nz)
    gap = (at[:, None] - at[None, :]) % nz
    ring = (2 * (gap == 0) + (gap == 1) + (gap == nz - 1)).astype(bf16)
    sizes = [snaps * part // sum(CHUNKS) for part in CHUNKS]
    chunks = len(sizes)
    blocks = [[None] * chunks for _ in range(groups)]
    coefs = None
    for c in range(chunks):
        own = pack(flow, field, sum(sizes[:c]), sizes[c], c == 0)
        lo = shift(own, "slab", 1)
        hi = shift(own, "slab", -1)
        before = [blocks[1][c - 1]] if c else []
        parts, made = sections(where, ring, coefs, own, lo, hi, groups, flow, before)
        coefs = coefs or made
        blocks[0][c] = parts[0]
        for k in range(1, groups):
            blocks[k][c] = swap(parts[k], "grp", k)
    flat = [blocks[k][c] for k in range(groups) for c in range(chunks)]
    keep, send = coupling(where, flat, groups, chunks)
    total = keep + swap(send, "slab", 1)
    bit = 2
    while bit < slabs:
        steps = [bit]
        if 2 * bit < slabs:
            steps += [2 * bit, 3 * bit]
        sent = total.astype(bf16)
        total = sum((swap(sent, "slab", s).astype(f32) for s in steps), total)
        bit *= 4
    sent = total.astype(bf16)
    total = sum((swap(sent, "grp", s).astype(f32) for s in range(1, groups)), total)
    mine = total * (1.0 / math.sqrt(rows * slabs * ny * nz))
    other = swap(mine, "slab", 1)
    outs = modes(where, mine, other, flat, groups, ny)
    outs = list(outs)
    for k in range(1, groups):
        outs[k] = swap(outs[k], "grp", k)
    return tuple(place(where, outs, groups))


def solution(mesh):
    return jax.shard_map(
        per_device,
        mesh=mesh,
        in_specs=(P("grp", None, "slab", None, None), P("slab", None, None)),
        out_specs=(P("grp", "slab", None, None), P("grp", "slab", None, None)),
        check_vma=False,
    )
```

```python
import functools
import math

import jax
import jax.numpy as jnp
from jax import lax
from jax.experimental import pallas as pl
from jax.experimental.pallas import tpu as pltpu
from jax.sharding import PartitionSpec as P

SECTIONS = 4
CHUNKS = (1, 1)
TALL = 32

diffuse_x = 0.35
diffuse_side = 0.05
damping = 0.5

VMEM_LIMIT = 48 * 1024 * 1024
vmem = pl.BlockSpec(memory_space=pltpu.VMEM)
smem = pl.BlockSpec(memory_space=pltpu.SMEM)
anywhere = pl.BlockSpec(memory_space=pl.ANY)
hbm = pl.BlockSpec(memory_space=pltpu.HBM)
f32 = jnp.float32
bf16 = jnp.bfloat16


def peer(index, step):
    return index ^ step


def swap(value, axis, step):
    count = lax.axis_size(axis)
    return lax.ppermute(value, axis, [(i, i ^ step) for i in range(count)])


def shift(value, axis, step):
    count = lax.axis_size(axis)
    return lax.ppermute(value, axis, [(i, (i + step) % count) for i in range(count)])


def pack_kernel(start, with_flow, flow_ref, field_ref, out, block, stage, sem):
    step, rows, ny, nz = block.shape
    copy = pltpu.make_async_copy(field_ref.at[pl.ds(start, step)], block, sem)
    copy.start()
    if with_flow:
        per = step // (rows * ny)
        left = flow_ref[...].reshape(rows * ny, nz)
        for p in range(3):
            part = left.astype(bf16)
            left = left - part.astype(f32)
            at = p % per * rows * ny
            out[rows * ny + p // per, at:at + rows * ny] = part
    copy.wait()
    for r in range(rows):
        stage[r % 2] = block[:, r].astype(f32).reshape(step * ny, nz)
        for y in range(ny):
            out[r * ny + y] = stage[r % 2, pl.ds(y, step, stride=ny), :].astype(bf16)


def pack(flow, field, start, step, with_flow):
    _, rows, ny, nz = field.shape
    extra = -(-3 // (step // (rows * ny))) if with_flow else 0
    return pl.pallas_call(
        functools.partial(pack_kernel, start, with_flow),
        out_shape=jax.ShapeDtypeStruct((rows * ny + extra, step, nz), bf16),
        in_specs=[vmem, hbm],
        out_specs=vmem,
        scratch_shapes=[
            pltpu.VMEM((step, rows, ny, nz), bf16),
            pltpu.VMEM((2, step * ny, nz), f32),
            pltpu.SemaphoreType.DMA(()),
        ],
        compiler_params=pltpu.CompilerParams(vmem_limit_bytes=VMEM_LIMIT),
        name="pack",
    )(flow, field)


def sections_kernel(groups, rows, ny, lead, where_ref, ring_ref, *rest):
    reach = SECTIONS
    total_rows = rows + 2 * reach
    me = where_ref[0]
    if lead:
        flow_ref, own_ref, lo_ref, hi_ref = rest[:4]
        outs = rest[4:4 + groups]
        plus, minus, flow_ext, done = rest[4 + groups:]
    else:
        plus, minus, own_ref, lo_ref, hi_ref, _ = rest[:6]
        outs = rest[6:6 + groups]
        done, = rest[6 + groups:]
    step, nz = own_ref.shape[1:]
    if lead:
        adj = (me == groups - 1).astype(jnp.int32)
        sign = jnp.where(me == groups - 1, f32(1.0), f32(-1.0))
        per = step // (rows * ny)

        def flow_of(ref):
            flow = None
            for p in (2, 1, 0):
                at = p % per * rows * ny
                part = ref[rows * ny + p // per, at:at + rows * ny].astype(f32)
                flow = part if flow is None else flow + part
            return flow.reshape(rows, ny, nz)

        flow_ext[0:reach] = flow_of(lo_ref)[rows - reach:]
        flow_ext[reach:reach + rows] = flow_ref[...]
        flow_ext[reach + rows:] = flow_of(hi_ref)[:reach]
        for e in range(1, total_rows - 1):
            plus[e] = diffuse_x + sign * flow_ext[e + adj]
            minus[e] = diffuse_x - sign * flow_ext[e - adj]
    ring = ring_ref[...]

    def entry(e, y):
        if e < reach:
            return lo_ref, (rows - reach + e) * ny + y
        if e < reach + rows:
            return own_ref, (e - reach) * ny + y
        return hi_ref, (e - reach - rows) * ny + y

    tall = math.gcd(step, TALL)

    def body(block, carry):
        at = pl.ds(pl.multiple_of(block * tall, tall), tall)

        def load(e):
            low = [ref[row, at, :] for ref, row in (entry(e, y) for y in range(ny))]
            return low, [part.astype(f32) for part in low]

        def advance(e, behind, here, ahead):
            low, mid = here
            side = jnp.dot(jnp.concatenate(low, axis=0), ring, preferred_element_type=f32)
            made = []
            for y in range(ny):
                total = side[y * tall:(y + 1) * tall] + (mid[(y + 1) % ny] + mid[(y - 1) % ny])
                total = diffuse_side * total + plus[e, y:y + 1, :] * ahead[1][y]
                total = total + minus[e, y:y + 1, :] * behind[1][y]
                made.append(total.astype(bf16))
            return made, [part.astype(f32) for part in made]

        held = [{} for _ in range(SECTIONS + 1)]
        for t in range(total_rows):
            held[0][t] = load(t)
            for s in range(1, SECTIONS + 1):
                e = t - s
                if s <= e < total_rows - s:
                    below = held[s - 1]
                    held[s][e] = advance(e, below[e - 1], below[e], below[e + 1])
                    del below[e - 1]
                    if s == SECTIONS:
                        for y in range(ny):
                            done[e - reach, y, at, :] = held[s][e][0][y]
        return carry

    lax.fori_loop(0, step // tall, body, 0)
    share = rows // groups
    for k in range(groups):
        for j in range(share):
            outs[k][j * ny:(j + 1) * ny] = done[peer(me, k) * share + j]


def sections(where, ring, coefs, own, lo, hi, groups, flow, before):
    rows, ny, nz = flow.shape
    step = own.shape[1]
    share = rows // groups
    total = rows + 2 * SECTIONS
    lead = coefs is None
    out = [jax.ShapeDtypeStruct((share * ny, step, nz), bf16)] * groups
    scratch = [pltpu.VMEM((rows, ny, step, nz), bf16)]
    if lead:
        out += [jax.ShapeDtypeStruct((total, ny, nz), f32)] * 2
        scratch = [pltpu.VMEM((total, ny, nz), f32)] + scratch
        coefs = [flow]
    outs = pl.pallas_call(
        functools.partial(sections_kernel, groups, rows, ny, lead),
        out_shape=out,
        in_specs=[smem] + [vmem] * (4 + len(coefs)) + [anywhere] * len(before),
        out_specs=[vmem] * len(out),
        scratch_shapes=scratch,
        compiler_params=pltpu.CompilerParams(vmem_limit_bytes=VMEM_LIMIT),
        cost_estimate=pl.CostEstimate(
            flops=8 * SECTIONS * step * total * ny * nz, bytes_accessed=8 * step * rows * ny * nz, transcendentals=0),
        name="sections",
    )(where, ring, *coefs, own, lo, hi, *before)
    return outs[:groups], outs[groups:]


def by_group(me, groups, action):
    for g in range(groups):
        pl.when(me == g)(functools.partial(action, g))


def coupling_kernel(groups, chunks, where_ref, *rest):
    blocks = rest[: groups * chunks]
    keep, send, scratch = rest[groups * chunks:]
    me, half = where_ref[0], where_ref[1]
    parts = blocks[0].shape[0]
    width = 2 if parts % 2 == 0 else 1
    snaps = scratch.shape[0]

    def action(mine):
        def wide(g, y):
            own = blocks[peer(mine, g) * chunks:(peer(mine, g) + 1) * chunks]
            return jnp.concatenate([
                jnp.concatenate([block[y + i] for block in own], axis=0) for i in range(width)
            ], axis=1)

        total = None
        for y in range(0, parts, width):
            direct = jnp.concatenate([wide(g, y) for g in range(groups - 1)], axis=0)
            term = lax.dot_general(wide(groups - 1, y), direct, (((1,), (1,)), ((), ())),
                                   preferred_element_type=f32)
            total = term if total is None else total + term
        scratch[...] = total

    by_group(me, groups, action)
    mid = snaps // 2
    keep[...] = scratch[pl.ds(pl.multiple_of(half * mid, mid), mid), :]
    send[...] = scratch[pl.ds(pl.multiple_of((1 - half) * mid, mid), mid), :]


def coupling(where, blocks, groups, chunks):
    snaps = sum(block.shape[1] for block in blocks[:chunks])
    wide = (groups - 1) * snaps
    return pl.pallas_call(
        functools.partial(coupling_kernel, groups, chunks),
        out_shape=[jax.ShapeDtypeStruct((snaps // 2, wide), f32)] * 2,
        in_specs=[smem] + [vmem] * (groups * chunks),
        out_specs=[vmem] * 2,
        scratch_shapes=[pltpu.VMEM((snaps, wide), f32)],
        compiler_params=pltpu.CompilerParams(vmem_limit_bytes=VMEM_LIMIT),
        name="coupling",
    )(where, *blocks)


def invert(system):
    size = system.shape[0]
    panels = [system[8 * i:8 * i + 8] for i in range(size // 8)]
    lane = lax.broadcasted_iota(jnp.int32, (8, size), 1)
    row = lax.broadcasted_iota(jnp.int32, (8, size), 0)

    def spread_lane(panel, j):
        return jnp.broadcast_to(panel[:, j:j + 1], (8, size))

    def spread_row(value, j):
        return jnp.broadcast_to(value[j:j + 1], (8, size))

    def small_inverse(a, b, d):
        det = a * d - b * b
        guess = pl.reciprocal(det, approx=True)
        guess = guess * (2.0 - det * guess)
        det = guess * (2.0 - det * guess)
        return d * det, -b * det, a * det

    for p in range(size // 8):
        for h in range(2):
            base = 8 * p + 4 * h
            lead = panels[p]
            cols = [spread_lane(lead, base + j) for j in range(4)]
            m = [[spread_row(cols[j], 4 * h + i) for j in range(4)] for i in range(4)]
            a0, a1, a2 = small_inverse(m[0][0], m[0][1], m[1][1])
            b00, b01, b10, b11 = m[0][2], m[0][3], m[1][2], m[1][3]
            x00, x01 = a0 * b00 + a1 * b10, a0 * b01 + a1 * b11
            x10, x11 = a1 * b00 + a2 * b10, a1 * b01 + a2 * b11
            s0 = m[2][2] - (b00 * x00 + b10 * x10)
            s1 = m[2][3] - (b00 * x01 + b10 * x11)
            s2 = m[3][3] - (b01 * x01 + b11 * x11)
            d0, d1, d2 = small_inverse(s0, s1, s2)
            y00, y01 = x00 * d0 + x01 * d1, x00 * d1 + x01 * d2
            y10, y11 = x10 * d0 + x11 * d1, x10 * d1 + x11 * d2
            inv = [
                [a0 + y00 * x00 + y01 * x01, a1 + y00 * x10 + y01 * x11, -y00, -y01],
                [None, a2 + y10 * x10 + y11 * x11, -y10, -y11],
                [None, None, d0, d1],
                [None, None, None, d2],
            ]
            for i in range(4):
                for j in range(i):
                    inv[i][j] = inv[j][i]
            rows4 = [spread_row(lead, 4 * h + i) for i in range(4)]
            for i in range(4):
                for j in range(4):
                    rows4[i] = jnp.where(lane == base + j, f32(1.0 if i == j else 0.0), rows4[i])
            new = [sum(inv[i][j] * rows4[j] for j in range(4)) for i in range(4)]
            block = (lane >= base) & (lane < base + 4)
            for q in range(size // 8):
                target = panels[q]
                kept = jnp.where(block, f32(0.0), target)
                if q == p:
                    factors = cols
                else:
                    factors = [spread_lane(target, base + j) for j in range(4)]
                out = kept - sum(factors[j] * new[j] for j in range(4))
                if q == p:
                    for i in range(4):
                        out = jnp.where(row == 4 * h + i, new[i], out)
                panels[q] = out
    return jnp.concatenate(panels, axis=0)


def modes_kernel(groups, chunks, where_ref, mine_ref, other_ref, *rest):
    blocks = rest[:groups * chunks]
    outs = rest[groups * chunks:groups * (chunks + 1)]
    coupling_ref, stage = rest[groups * (chunks + 1):]
    me, half = where_ref[0], where_ref[1]
    mid = mine_ref.shape[0]
    snaps = 2 * mid
    parts = blocks[0].shape[0]
    coupling_ref[pl.ds(pl.multiple_of(half * mid, mid), mid), :] = mine_ref[...]
    coupling_ref[pl.ds(pl.multiple_of((1 - half) * mid, mid), mid), :] = other_ref[...]
    coupled = coupling_ref[...]
    gram = lax.dot_general(coupled, coupled, (((1,), (1,)), ((), ())),
                           precision=lax.Precision.HIGHEST, preferred_element_type=f32)
    r = lax.broadcasted_iota(jnp.int32, (snaps, snaps), 0)
    c = lax.broadcasted_iota(jnp.int32, (snaps, snaps), 1)
    diagonal = jnp.where(r == c, gram, 0.0)
    energy = jnp.sum(jnp.sum(diagonal, axis=0, keepdims=True), axis=1, keepdims=True) / snaps
    system = gram / energy + jnp.where(r == c, f32(damping), f32(0.0))
    inverse = invert(system)
    weights = jnp.dot(inverse, coupled, precision=lax.Precision.HIGHEST,
                      preferred_element_type=f32) / jnp.sqrt(energy)
    weights = weights.astype(bf16)
    inverse = inverse.astype(bf16)
    share = snaps // groups
    ny = outs[0].shape[3]
    layers = parts // ny

    def action(mine):
        def group(g, at):
            return [block[at] for block in blocks[peer(mine, g) * chunks:(peer(mine, g) + 1) * chunks]]

        for layer in range(layers):
            for y in range(ny):
                at = layer * ny + y
                rows = pl.ds(y, snaps, stride=ny)
                direct = jnp.concatenate(
                    [part for g in range(groups - 1) for part in group(g, at)], axis=0)
                adjoint = jnp.concatenate(group(groups - 1, at), axis=0)
                stage[0, layer, rows, :] = jnp.dot(weights, direct, preferred_element_type=f32)
                stage[1, layer, rows, :] = jnp.dot(inverse, adjoint, preferred_element_type=f32)

    by_group(me, groups, action)
    for k in range(groups):
        start = pl.multiple_of(peer(me, k) * (share * ny), share * ny)
        for which in range(2):
            for layer in range(layers):
                value = stage[which, layer, pl.ds(start, share * ny), :]
                outs[k][which, :, layer] = value.reshape(share, ny, value.shape[1]).astype(bf16)


def modes(where, mine, other, blocks, groups, ny):
    chunks = len(blocks) // groups
    parts, _, nz = blocks[0].shape
    snaps = 2 * mine.shape[0]
    layers = parts // ny
    share = snaps // groups
    return pl.pallas_call(
        functools.partial(modes_kernel, groups, chunks),
        out_shape=[jax.ShapeDtypeStruct((2, share, layers, ny, nz), bf16)] * groups,
        in_specs=[smem, vmem, vmem] + [vmem] * len(blocks),
        out_specs=[vmem] * groups,
        scratch_shapes=[pltpu.VMEM((snaps, mine.shape[1]), f32),
                        pltpu.VMEM((2, layers, snaps * ny, nz), f32)],
        compiler_params=pltpu.CompilerParams(vmem_limit_bytes=VMEM_LIMIT),
        name="modes",
    )(where, mine, other, *blocks)


def place_kernel(groups, where_ref, *rest):
    blocks = rest[:groups]
    outs = rest[groups:]
    me = where_ref[0]
    layers = blocks[0].shape[2]
    for k in range(groups):
        for which in range(2):
            for layer in range(layers):
                outs[which][:, peer(me, k) * layers + layer] = blocks[k][which, :, layer]


def place(where, blocks, groups):
    _, share, layers, ny, nz = blocks[0].shape
    out = jax.ShapeDtypeStruct((share, layers * groups, ny, nz), bf16)
    return pl.pallas_call(
        functools.partial(place_kernel, groups),
        out_shape=[out, out],
        in_specs=[smem] + [vmem] * groups,
        out_specs=[vmem] * 2,
        compiler_params=pltpu.CompilerParams(vmem_limit_bytes=8 * 1024 * 1024),
        name="place",
    )(where, *blocks)


def per_device(snapshots, base_flow):
    field = snapshots[0]
    snaps, rows, ny, nz = field.shape
    groups = lax.axis_size("grp")
    slabs = lax.axis_size("slab")
    me = lax.axis_index("grp")
    half = lax.axis_index("slab") % 2
    where = jnp.stack([me, half]).astype(jnp.int32)
    flow = 0.5 * base_flow
    at = jnp.arange(nz)
    gap = (at[:, None] - at[None, :]) % nz
    ring = (2 * (gap == 0) + (gap == 1) + (gap == nz - 1)).astype(bf16)
    sizes = [snaps * part // sum(CHUNKS) for part in CHUNKS]
    chunks = len(sizes)
    blocks = [[None] * chunks for _ in range(groups)]
    coefs = None
    for c in range(chunks):
        own = pack(flow, field, sum(sizes[:c]), sizes[c], c == 0)
        lo = shift(own, "slab", 1)
        hi = shift(own, "slab", -1)
        before = [blocks[1][c - 1]] if c else []
        parts, made = sections(where, ring, coefs, own, lo, hi, groups, flow, before)
        coefs = coefs or made
        blocks[0][c] = parts[0]
        for k in range(1, groups):
            blocks[k][c] = swap(parts[k], "grp", k)
    flat = [blocks[k][c] for k in range(groups) for c in range(chunks)]
    keep, send = coupling(where, flat, groups, chunks)
    total = keep + swap(send, "slab", 1)
    bit = 2
    while bit < slabs:
        steps = [bit]
        if 2 * bit < slabs:
            steps += [2 * bit, 3 * bit]
        sent = total.astype(bf16)
        total = sum((swap(sent, "slab", s).astype(f32) for s in steps), total)
        bit *= 4
    sent = total.astype(bf16)
    total = sum((swap(sent, "grp", s).astype(f32) for s in range(1, groups)), total)
    mine = total * (1.0 / math.sqrt(rows * slabs * ny * nz))
    other = swap(mine, "slab", 1)
    outs = modes(where, mine, other, flat, groups, ny)
    outs = list(outs)
    for k in range(1, groups):
        outs[k] = swap(outs[k], "grp", k)
    return tuple(place(where, outs, groups))


def solution(mesh):
    return jax.shard_map(
        per_device,
        mesh=mesh,
        in_specs=(P("grp", None, "slab", None, None), P("slab", None, None)),
        out_specs=(P("grp", "slab", None, None), P("grp", "slab", None, None)),
        check_vma=False,
    )
```

```python
import functools
import math

import jax
import jax.numpy as jnp
from jax import lax
from jax.experimental import pallas as pl
from jax.experimental.pallas import tpu as pltpu
from jax.sharding import PartitionSpec as P

SECTIONS = 4
CHUNKS = (1, 1)
TALL = 32

diffuse_x = 0.35
diffuse_side = 0.05
damping = 0.5

VMEM_LIMIT = 48 * 1024 * 1024
vmem = pl.BlockSpec(memory_space=pltpu.VMEM)
smem = pl.BlockSpec(memory_space=pltpu.SMEM)
anywhere = pl.BlockSpec(memory_space=pl.ANY)
hbm = pl.BlockSpec(memory_space=pltpu.HBM)
f32 = jnp.float32
bf16 = jnp.bfloat16


def peer(index, step):
    return index ^ step


def swap(value, axis, step):
    count = lax.axis_size(axis)
    return lax.ppermute(value, axis, [(i, i ^ step) for i in range(count)])


def shift(value, axis, step):
    count = lax.axis_size(axis)
    return lax.ppermute(value, axis, [(i, (i + step) % count) for i in range(count)])


def pack_kernel(start, with_flow, flow_ref, field_ref, out, block, stage, sem):
    step, rows, ny, nz = block.shape
    copy = pltpu.make_async_copy(field_ref.at[pl.ds(start, step)], block, sem)
    copy.start()
    if with_flow:
        per = step // (rows * ny)
        left = flow_ref[...].reshape(rows * ny, nz)
        for p in range(3):
            part = left.astype(bf16)
            left = left - part.astype(f32)
            at = p % per * rows * ny
            out[rows * ny + p // per, at:at + rows * ny] = part
    copy.wait()
    for r in range(rows):
        stage[r % 2] = block[:, r].astype(f32).reshape(step * ny, nz)
        for y in range(ny):
            out[r * ny + y] = stage[r % 2, pl.ds(y, step, stride=ny), :].astype(bf16)


def pack(flow, field, start, step, with_flow):
    _, rows, ny, nz = field.shape
    extra = -(-3 // (step // (rows * ny))) if with_flow else 0
    return pl.pallas_call(
        functools.partial(pack_kernel, start, with_flow),
        out_shape=jax.ShapeDtypeStruct((rows * ny + extra, step, nz), bf16),
        in_specs=[vmem, hbm],
        out_specs=vmem,
        scratch_shapes=[
            pltpu.VMEM((step, rows, ny, nz), bf16),
            pltpu.VMEM((2, step * ny, nz), f32),
            pltpu.SemaphoreType.DMA(()),
        ],
        compiler_params=pltpu.CompilerParams(vmem_limit_bytes=VMEM_LIMIT),
        name="pack",
    )(flow, field)


def sections_kernel(groups, rows, ny, lead, where_ref, ring_ref, *rest):
    reach = SECTIONS
    total_rows = rows + 2 * reach
    me = where_ref[0]
    if lead:
        flow_ref, own_ref, lo_ref, hi_ref = rest[:4]
        outs = rest[4:4 + groups]
        plus, minus, flow_ext, done = rest[4 + groups:]
    else:
        plus, minus, own_ref, lo_ref, hi_ref, _ = rest[:6]
        outs = rest[6:6 + groups]
        done, = rest[6 + groups:]
    step, nz = own_ref.shape[1:]
    if lead:
        adj = (me == groups - 1).astype(jnp.int32)
        sign = jnp.where(me == groups - 1, f32(1.0), f32(-1.0))
        per = step // (rows * ny)

        def flow_of(ref):
            flow = None
            for p in (2, 1, 0):
                at = p % per * rows * ny
                part = ref[rows * ny + p // per, at:at + rows * ny].astype(f32)
                flow = part if flow is None else flow + part
            return flow.reshape(rows, ny, nz)

        flow_ext[0:reach] = flow_of(lo_ref)[rows - reach:]
        flow_ext[reach:reach + rows] = flow_ref[...]
        flow_ext[reach + rows:] = flow_of(hi_ref)[:reach]
        for e in range(1, total_rows - 1):
            plus[e] = diffuse_x + sign * flow_ext[e + adj]
            minus[e] = diffuse_x - sign * flow_ext[e - adj]
    ring = ring_ref[...]

    def entry(e, y):
        if e < reach:
            return lo_ref, (rows - reach + e) * ny + y
        if e < reach + rows:
            return own_ref, (e - reach) * ny + y
        return hi_ref, (e - reach - rows) * ny + y

    tall = math.gcd(step, TALL)

    def body(block, carry):
        at = pl.ds(pl.multiple_of(block * tall, tall), tall)

        def load(e):
            low = [ref[row, at, :] for ref, row in (entry(e, y) for y in range(ny))]
            return low, [part.astype(f32) for part in low]

        def advance(e, behind, here, ahead):
            low, mid = here
            side = jnp.dot(jnp.concatenate(low, axis=0), ring, preferred_element_type=f32)
            made = []
            for y in range(ny):
                total = side[y * tall:(y + 1) * tall] + (mid[(y + 1) % ny] + mid[(y - 1) % ny])
                total = diffuse_side * total + plus[e, y:y + 1, :] * ahead[1][y]
                total = total + minus[e, y:y + 1, :] * behind[1][y]
                made.append(total.astype(bf16))
            return made, [part.astype(f32) for part in made]

        held = [{} for _ in range(SECTIONS + 1)]
        for t in range(total_rows):
            held[0][t] = load(t)
            for s in range(1, SECTIONS + 1):
                e = t - s
                if s <= e < total_rows - s:
                    below = held[s - 1]
                    held[s][e] = advance(e, below[e - 1], below[e], below[e + 1])
                    del below[e - 1]
                    if s == SECTIONS:
                        for y in range(ny):
                            done[e - reach, y, at, :] = held[s][e][0][y]
        return carry

    lax.fori_loop(0, step // tall, body, 0)
    share = rows // groups
    for k in range(groups):
        for j in range(share):
            outs[k][j * ny:(j + 1) * ny] = done[peer(me, k) * share + j]


def sections(where, ring, coefs, own, lo, hi, groups, flow, before):
    rows, ny, nz = flow.shape
    step = own.shape[1]
    share = rows // groups
    total = rows + 2 * SECTIONS
    lead = coefs is None
    out = [jax.ShapeDtypeStruct((share * ny, step, nz), bf16)] * groups
    scratch = [pltpu.VMEM((rows, ny, step, nz), bf16)]
    if lead:
        out += [jax.ShapeDtypeStruct((total, ny, nz), f32)] * 2
        scratch = [pltpu.VMEM((total, ny, nz), f32)] + scratch
        coefs = [flow]
    outs = pl.pallas_call(
        functools.partial(sections_kernel, groups, rows, ny, lead),
        out_shape=out,
        in_specs=[smem] + [vmem] * (4 + len(coefs)) + [anywhere] * len(before),
        out_specs=[vmem] * len(out),
        scratch_shapes=scratch,
        compiler_params=pltpu.CompilerParams(vmem_limit_bytes=VMEM_LIMIT),
        cost_estimate=pl.CostEstimate(
            flops=8 * SECTIONS * step * total * ny * nz, bytes_accessed=8 * step * rows * ny * nz, transcendentals=0),
        name="sections",
    )(where, ring, *coefs, own, lo, hi, *before)
    return outs[:groups], outs[groups:]


def by_group(me, groups, action):
    for g in range(groups):
        pl.when(me == g)(functools.partial(action, g))


def coupling_kernel(groups, chunks, where_ref, *rest):
    blocks = rest[: groups * chunks]
    keep, send, scratch = rest[groups * chunks:]
    me, half = where_ref[0], where_ref[1]
    parts = blocks[0].shape[0]
    width = 2 if parts % 2 == 0 else 1
    snaps = scratch.shape[0]

    def action(mine):
        def wide(g, y):
            own = blocks[peer(mine, g) * chunks:(peer(mine, g) + 1) * chunks]
            return jnp.concatenate([
                jnp.concatenate([block[y + i] for block in own], axis=0) for i in range(width)
            ], axis=1)

        total = None
        for y in range(0, parts, width):
            direct = jnp.concatenate([wide(g, y) for g in range(groups - 1)], axis=0)
            term = lax.dot_general(wide(groups - 1, y), direct, (((1,), (1,)), ((), ())),
                                   preferred_element_type=f32)
            total = term if total is None else total + term
        scratch[...] = total

    by_group(me, groups, action)
    mid = snaps // 2
    keep[...] = scratch[pl.ds(pl.multiple_of(half * mid, mid), mid), :]
    send[...] = scratch[pl.ds(pl.multiple_of((1 - half) * mid, mid), mid), :]


def coupling(where, blocks, groups, chunks):
    snaps = sum(block.shape[1] for block in blocks[:chunks])
    wide = (groups - 1) * snaps
    return pl.pallas_call(
        functools.partial(coupling_kernel, groups, chunks),
        out_shape=[jax.ShapeDtypeStruct((snaps // 2, wide), f32)] * 2,
        in_specs=[smem] + [vmem] * (groups * chunks),
        out_specs=[vmem] * 2,
        scratch_shapes=[pltpu.VMEM((snaps, wide), f32)],
        compiler_params=pltpu.CompilerParams(vmem_limit_bytes=VMEM_LIMIT),
        name="coupling",
    )(where, *blocks)


def invert(system, held):
    size = system.shape[0]
    count = size // 8
    panels = [system[8 * i:8 * i + 8] for i in range(count)]
    lane = lax.broadcasted_iota(jnp.int32, (8, size), 1)
    row = lax.broadcasted_iota(jnp.int32, (8, size), 0)

    def spread(panel, j):
        return jnp.broadcast_to(panel[:, j:j + 1], (8, size))

    def reciprocal(value):
        guess = pl.reciprocal(value, approx=True)
        guess = guess * (2.0 - value * guess)
        return guess * (2.0 - value * guess)

    for p in range(count):
        base, slot = 8 * p, p % 2
        lead = panels[p]
        for j in range(8):
            held[slot, 8 * j:8 * j + 8, :] = spread(lead, base + j)
        held[slot, 64:72, :] = lead

        def row_of(at, slot=slot):
            return jnp.broadcast_to(held[slot, at:at + 1, :], (8, size))

        m = {(i, j): row_of(8 * j + i) for j in range(8) for i in range(j + 1)}
        block = (lane >= base) & (lane < base + 8)
        r = [jnp.where(lane == base + i, f32(1.0), jnp.where(block, f32(0.0), row_of(64 + i)))
             for i in range(8)]
        blocks, x = [], {}
        for i in range(0, 8, 2):
            a, b, d = m[i, i], m[i, i + 1], m[i + 1, i + 1]
            det = reciprocal(a * d - b * b)
            v0, v1, v2 = d * det, -b * det, a * det
            blocks.append((v0, v1, v2))
            for j in range(i + 2, 8):
                x[i, j] = v0 * m[i, j] + v1 * m[i + 1, j]
                x[i + 1, j] = v1 * m[i, j] + v2 * m[i + 1, j]
            for j in range(i + 2, 8):
                for h in range(i + 2, j + 1):
                    m[h, j] = m[h, j] - (m[i, h] * x[i, j] + m[i + 1, h] * x[i + 1, j])
            for j in range(i + 2, 8):
                r[j] = r[j] - (x[i, j] * r[i] + x[i + 1, j] * r[i + 1])
        new = [None] * 8
        for i in (6, 4, 2, 0):
            v0, v1, v2 = blocks[i // 2]
            top = v0 * r[i] + v1 * r[i + 1]
            low = v1 * r[i] + v2 * r[i + 1]
            for j in range(i + 2, 8):
                top = top - x[i, j] * new[j]
                low = low - x[i + 1, j] * new[j]
            new[i], new[i + 1] = top, low
        for q in [(p + 1 + z) % count for z in range(count)]:
            target = panels[q]
            if q == p:
                out = new[0]
                for i in range(1, 8):
                    out = jnp.where(row == i, new[i], out)
            else:
                out = jnp.where(block, f32(0.0), target)
                out = out - sum(spread(target, base + j) * new[j] for j in range(8))
            panels[q] = out
    return jnp.concatenate(panels, axis=0)


def modes_kernel(groups, chunks, where_ref, mine_ref, other_ref, *rest):
    blocks = rest[:groups * chunks]
    outs = rest[groups * chunks:groups * (chunks + 1)]
    coupling_ref, stage, held = rest[groups * (chunks + 1):]
    me, half = where_ref[0], where_ref[1]
    mid = mine_ref.shape[0]
    snaps = 2 * mid
    parts = blocks[0].shape[0]
    coupling_ref[pl.ds(pl.multiple_of(half * mid, mid), mid), :] = mine_ref[...]
    coupling_ref[pl.ds(pl.multiple_of((1 - half) * mid, mid), mid), :] = other_ref[...]
    coupled = coupling_ref[...]
    gram = lax.dot_general(coupled, coupled, (((1,), (1,)), ((), ())),
                           precision=lax.Precision.HIGHEST, preferred_element_type=f32)
    r = lax.broadcasted_iota(jnp.int32, (snaps, snaps), 0)
    c = lax.broadcasted_iota(jnp.int32, (snaps, snaps), 1)
    diagonal = jnp.where(r == c, gram, 0.0)
    energy = jnp.sum(jnp.sum(diagonal, axis=0, keepdims=True), axis=1, keepdims=True) / snaps
    system = gram / energy + jnp.where(r == c, f32(damping), f32(0.0))
    inverse = invert(system, held)
    weights = jnp.dot(inverse, coupled, precision=lax.Precision.HIGHEST,
                      preferred_element_type=f32) / jnp.sqrt(energy)
    weights = weights.astype(bf16)
    inverse = inverse.astype(bf16)
    share = snaps // groups
    ny = outs[0].shape[3]
    layers = parts // ny

    def action(mine):
        def group(g, at):
            return [block[at] for block in blocks[peer(mine, g) * chunks:(peer(mine, g) + 1) * chunks]]

        for layer in range(layers):
            for y in range(ny):
                at = layer * ny + y
                rows = pl.ds(y, snaps, stride=ny)
                direct = jnp.concatenate(
                    [part for g in range(groups - 1) for part in group(g, at)], axis=0)
                adjoint = jnp.concatenate(group(groups - 1, at), axis=0)
                stage[0, layer, rows, :] = jnp.dot(weights, direct, preferred_element_type=f32)
                stage[1, layer, rows, :] = jnp.dot(inverse, adjoint, preferred_element_type=f32)

    by_group(me, groups, action)
    for k in range(groups):
        start = pl.multiple_of(peer(me, k) * (share * ny), share * ny)
        for which in range(2):
            for layer in range(layers):
                value = stage[which, layer, pl.ds(start, share * ny), :]
                outs[k][which, :, layer] = value.reshape(share, ny, value.shape[1]).astype(bf16)


def modes(where, mine, other, blocks, groups, ny):
    chunks = len(blocks) // groups
    parts, _, nz = blocks[0].shape
    snaps = 2 * mine.shape[0]
    layers = parts // ny
    share = snaps // groups
    return pl.pallas_call(
        functools.partial(modes_kernel, groups, chunks),
        out_shape=[jax.ShapeDtypeStruct((2, share, layers, ny, nz), bf16)] * groups,
        in_specs=[smem, vmem, vmem] + [vmem] * len(blocks),
        out_specs=[vmem] * groups,
        scratch_shapes=[pltpu.VMEM((snaps, mine.shape[1]), f32),
                        pltpu.VMEM((2, layers, snaps * ny, nz), f32),
                        pltpu.VMEM((2, 72, snaps), f32)],
        compiler_params=pltpu.CompilerParams(vmem_limit_bytes=VMEM_LIMIT),
        name="modes",
    )(where, mine, other, *blocks)


def place_kernel(groups, where_ref, *rest):
    blocks = rest[:groups]
    outs = rest[groups:]
    me = where_ref[0]
    layers = blocks[0].shape[2]
    for k in range(groups):
        for which in range(2):
            for layer in range(layers):
                outs[which][:, peer(me, k) * layers + layer] = blocks[k][which, :, layer]


def place(where, blocks, groups):
    _, share, layers, ny, nz = blocks[0].shape
    out = jax.ShapeDtypeStruct((share, layers * groups, ny, nz), bf16)
    return pl.pallas_call(
        functools.partial(place_kernel, groups),
        out_shape=[out, out],
        in_specs=[smem] + [vmem] * groups,
        out_specs=[vmem] * 2,
        compiler_params=pltpu.CompilerParams(vmem_limit_bytes=8 * 1024 * 1024),
        name="place",
    )(where, *blocks)


def per_device(snapshots, base_flow):
    field = snapshots[0]
    snaps, rows, ny, nz = field.shape
    groups = lax.axis_size("grp")
    slabs = lax.axis_size("slab")
    me = lax.axis_index("grp")
    half = lax.axis_index("slab") % 2
    where = jnp.stack([me, half]).astype(jnp.int32)
    flow = 0.5 * base_flow
    at = jnp.arange(nz)
    gap = (at[:, None] - at[None, :]) % nz
    ring = (2 * (gap == 0) + (gap == 1) + (gap == nz - 1)).astype(bf16)
    sizes = [snaps * part // sum(CHUNKS) for part in CHUNKS]
    chunks = len(sizes)
    blocks = [[None] * chunks for _ in range(groups)]
    coefs = None
    for c in range(chunks):
        own = pack(flow, field, sum(sizes[:c]), sizes[c], c == 0)
        lo = shift(own, "slab", 1)
        hi = shift(own, "slab", -1)
        before = [blocks[1][c - 1]] if c else []
        parts, made = sections(where, ring, coefs, own, lo, hi, groups, flow, before)
        coefs = coefs or made
        blocks[0][c] = parts[0]
        for k in range(1, groups):
            blocks[k][c] = swap(parts[k], "grp", k)
    flat = [blocks[k][c] for k in range(groups) for c in range(chunks)]
    keep, send = coupling(where, flat, groups, chunks)
    total = keep + swap(send, "slab", 1)
    bit = 2
    while bit < slabs:
        steps = [bit]
        if 2 * bit < slabs:
            steps += [2 * bit, 3 * bit]
        sent = total.astype(bf16)
        total = sum((swap(sent, "slab", s).astype(f32) for s in steps), total)
        bit *= 4
    sent = total.astype(bf16)
    total = sum((swap(sent, "grp", s).astype(f32) for s in range(1, groups)), total)
    mine = total * (1.0 / math.sqrt(rows * slabs * ny * nz))
    other = swap(mine, "slab", 1)
    outs = modes(where, mine, other, flat, groups, ny)
    outs = list(outs)
    for k in range(1, groups):
        outs[k] = swap(outs[k], "grp", k)
    return tuple(place(where, outs, groups))


def solution(mesh):
    return jax.shard_map(
        per_device,
        mesh=mesh,
        in_specs=(P("grp", None, "slab", None, None), P("slab", None, None)),
        out_specs=(P("grp", "slab", None, None), P("grp", "slab", None, None)),
        check_vma=False,
    )
```

```python
import functools
import math

import jax
import jax.numpy as jnp
from jax import lax
from jax.experimental import pallas as pl
from jax.experimental.pallas import tpu as pltpu
from jax.sharding import PartitionSpec as P

SECTIONS = 4
CHUNKS = (1, 1)
TALL = 32
TERMS = 2

diffuse_x = 0.35
diffuse_side = 0.05
damping = 0.5

VMEM_LIMIT = 48 * 1024 * 1024
vmem = pl.BlockSpec(memory_space=pltpu.VMEM)
smem = pl.BlockSpec(memory_space=pltpu.SMEM)
anywhere = pl.BlockSpec(memory_space=pl.ANY)
hbm = pl.BlockSpec(memory_space=pltpu.HBM)
f32 = jnp.float32
bf16 = jnp.bfloat16


def peer(index, step):
    return index ^ step


def swap(value, axis, step):
    count = lax.axis_size(axis)
    return lax.ppermute(value, axis, [(i, i ^ step) for i in range(count)])


def swap_outer(value, axis):
    count = lax.axis_size(axis)
    return lax.ppermute(value, axis, [(i, (i + 2 * (i % 2) - 1) % count) for i in range(count)])


def pack_kernel(start, with_flow, flow_ref, field_ref, *rest):
    out, block, stage, sem = rest[-4:]
    step, rows, ny, nz = block.shape
    copy = pltpu.make_async_copy(field_ref.at[pl.ds(start, step)], block, sem)
    copy.start()
    if with_flow:
        per = step // (rows * ny)
        left = flow_ref[...].reshape(rows * ny, nz)
        for p in range(TERMS):
            part = left.astype(bf16)
            left = left - part.astype(f32)
            at = p % per * rows * ny
            out[rows * ny + p // per, at:at + rows * ny] = part
    copy.wait()
    for r in range(rows):
        stage[r % 2] = block[:, r].astype(f32).reshape(step * ny, nz)
        for y in range(ny):
            out[r * ny + y] = stage[r % 2, pl.ds(y, step, stride=ny), :].astype(bf16)


def pack(flow, field, start, step, with_flow, before):
    _, rows, ny, nz = field.shape
    extra = -(-TERMS // (step // (rows * ny))) if with_flow else 0
    return pl.pallas_call(
        functools.partial(pack_kernel, start, with_flow),
        out_shape=jax.ShapeDtypeStruct((rows * ny + extra, step, nz), bf16),
        in_specs=[vmem, hbm] + [anywhere] * len(before),
        out_specs=vmem,
        scratch_shapes=[
            pltpu.VMEM((step, rows, ny, nz), bf16),
            pltpu.VMEM((2, step * ny, nz), f32),
            pltpu.SemaphoreType.DMA(()),
        ],
        compiler_params=pltpu.CompilerParams(vmem_limit_bytes=VMEM_LIMIT),
        name="pack",
    )(flow, field, *before)


def sections_kernel(groups, rows, ny, lead, where_ref, ring_ref, *rest):
    reach = SECTIONS
    total_rows = rows + 2 * reach
    me = where_ref[0]
    low_core = where_ref[1] == 0
    if lead:
        flow_ref, own_ref, inner_ref, outer_ref = rest[:4]
        outs = rest[4:4 + groups]
        plus, minus, flow_ext, done = rest[4 + groups:]
    else:
        plus, minus, own_ref, inner_ref, outer_ref, _ = rest[:6]
        outs = rest[6:6 + groups]
        done, = rest[6 + groups:]
    step, nz = own_ref.shape[1:]
    if lead:
        adj = (me == groups - 1).astype(jnp.int32)
        sign = jnp.where(me == groups - 1, f32(1.0), f32(-1.0))
        per = step // (rows * ny)

        def flow_of(ref):
            flow = None
            for p in reversed(range(TERMS)):
                at = p % per * rows * ny
                part = ref[rows * ny + p // per, at:at + rows * ny].astype(f32)
                flow = part if flow is None else flow + part
            return flow.reshape(rows, ny, nz)

        inner, outer = flow_of(inner_ref), flow_of(outer_ref)
        flow_ext[0:reach] = jnp.where(low_core, outer, inner)[rows - reach:]
        flow_ext[reach:reach + rows] = flow_ref[...]
        flow_ext[reach + rows:] = jnp.where(low_core, inner, outer)[:reach]
        for e in range(1, total_rows - 1):
            plus[e] = diffuse_x + sign * flow_ext[e + adj]
            minus[e] = diffuse_x - sign * flow_ext[e - adj]
    ring = ring_ref[...]

    def entry(e, y, at):
        if e < reach:
            row = (rows - reach + e) * ny + y
            return jnp.where(low_core, outer_ref[row, at, :], inner_ref[row, at, :])
        if e < reach + rows:
            return own_ref[(e - reach) * ny + y, at, :]
        row = (e - reach - rows) * ny + y
        return jnp.where(low_core, inner_ref[row, at, :], outer_ref[row, at, :])

    tall = math.gcd(step, TALL)

    def body(block, carry):
        at = pl.ds(pl.multiple_of(block * tall, tall), tall)

        def load(e):
            low = [entry(e, y, at) for y in range(ny)]
            return low, [part.astype(f32) for part in low]

        def advance(e, behind, here, ahead):
            low, mid = here
            side = jnp.dot(jnp.concatenate(low, axis=0), ring, preferred_element_type=f32)
            made = []
            for y in range(ny):
                total = side[y * tall:(y + 1) * tall] + (mid[(y + 1) % ny] + mid[(y - 1) % ny])
                total = diffuse_side * total + plus[e, y:y + 1, :] * ahead[1][y]
                total = total + minus[e, y:y + 1, :] * behind[1][y]
                made.append(total.astype(bf16))
            return made, [part.astype(f32) for part in made]

        held = [{} for _ in range(SECTIONS + 1)]
        for t in range(total_rows):
            held[0][t] = load(t)
            for s in range(1, SECTIONS + 1):
                e = t - s
                if s <= e < total_rows - s:
                    below = held[s - 1]
                    held[s][e] = advance(e, below[e - 1], below[e], below[e + 1])
                    del below[e - 1]
                    if s == SECTIONS:
                        for y in range(ny):
                            done[e - reach, y, at, :] = held[s][e][0][y]
        return carry

    lax.fori_loop(0, step // tall, body, 0)
    share = rows // groups
    for k in range(groups):
        for j in range(share):
            outs[k][j * ny:(j + 1) * ny] = done[peer(me, k) * share + j]


def sections(where, ring, coefs, own, inner, outer, groups, flow, before):
    rows, ny, nz = flow.shape
    step = own.shape[1]
    share = rows // groups
    total = rows + 2 * SECTIONS
    lead = coefs is None
    out = [jax.ShapeDtypeStruct((share * ny, step, nz), bf16)] * groups
    scratch = [pltpu.VMEM((rows, ny, step, nz), bf16)]
    if lead:
        out += [jax.ShapeDtypeStruct((total, ny, nz), f32)] * 2
        scratch = [pltpu.VMEM((total, ny, nz), f32)] + scratch
        coefs = [flow]
    outs = pl.pallas_call(
        functools.partial(sections_kernel, groups, rows, ny, lead),
        out_shape=out,
        in_specs=[smem] + [vmem] * (4 + len(coefs)) + [anywhere] * len(before),
        out_specs=[vmem] * len(out),
        scratch_shapes=scratch,
        compiler_params=pltpu.CompilerParams(vmem_limit_bytes=VMEM_LIMIT),
        cost_estimate=pl.CostEstimate(
            flops=8 * SECTIONS * step * total * ny * nz, bytes_accessed=8 * step * rows * ny * nz, transcendentals=0),
        name="sections",
    )(where, ring, *coefs, own, inner, outer, *before)
    return outs[:groups], outs[groups:]


def by_group(me, groups, action):
    for g in range(groups):
        pl.when(me == g)(functools.partial(action, g))


def coupling_kernel(groups, chunks, where_ref, *rest):
    blocks = rest[: groups * chunks]
    keep, send, scratch = rest[groups * chunks:]
    me, half = where_ref[0], where_ref[1]
    parts = blocks[0].shape[0]
    width = 2 if parts % 2 == 0 else 1
    snaps = scratch.shape[0]

    def action(mine):
        def wide(g, y):
            own = blocks[peer(mine, g) * chunks:(peer(mine, g) + 1) * chunks]
            return jnp.concatenate([
                jnp.concatenate([block[y + i] for block in own], axis=0) for i in range(width)
            ], axis=1)

        total = None
        for y in range(0, parts, width):
            direct = jnp.concatenate([wide(g, y) for g in range(groups - 1)], axis=0)
            term = lax.dot_general(wide(groups - 1, y), direct, (((1,), (1,)), ((), ())),
                                   preferred_element_type=f32)
            total = term if total is None else total + term
        scratch[...] = total

    by_group(me, groups, action)
    mid = snaps // 2
    keep[...] = scratch[pl.ds(pl.multiple_of(half * mid, mid), mid), :]
    send[...] = scratch[pl.ds(pl.multiple_of((1 - half) * mid, mid), mid), :]


def coupling(where, blocks, groups, chunks):
    snaps = sum(block.shape[1] for block in blocks[:chunks])
    wide = (groups - 1) * snaps
    return pl.pallas_call(
        functools.partial(coupling_kernel, groups, chunks),
        out_shape=[jax.ShapeDtypeStruct((snaps // 2, wide), f32)] * 2,
        in_specs=[smem] + [vmem] * (groups * chunks),
        out_specs=[vmem] * 2,
        scratch_shapes=[pltpu.VMEM((snaps, wide), f32)],
        compiler_params=pltpu.CompilerParams(vmem_limit_bytes=VMEM_LIMIT),
        name="coupling",
    )(where, *blocks)


def invert(system, held):
    size = system.shape[0]
    count = size // 8
    panels = [system[8 * i:8 * i + 8] for i in range(count)]
    lane = lax.broadcasted_iota(jnp.int32, (8, size), 1)
    row = lax.broadcasted_iota(jnp.int32, (8, size), 0)

    def spread(panel, j):
        return jnp.broadcast_to(panel[:, j:j + 1], (8, size))

    def reciprocal(value):
        guess = pl.reciprocal(value, approx=True)
        guess = guess * (2.0 - value * guess)
        return guess * (2.0 - value * guess)

    for p in range(count):
        base, slot = 8 * p, p % 2
        lead = panels[p]
        for j in range(8):
            held[slot, 8 * j:8 * j + 8, :] = spread(lead, base + j)
        held[slot, 64:72, :] = lead

        def row_of(at, slot=slot):
            return jnp.broadcast_to(held[slot, at:at + 1, :], (8, size))

        m = {(i, j): row_of(8 * j + i) for j in range(8) for i in range(j + 1)}
        block = (lane >= base) & (lane < base + 8)
        r = [jnp.where(lane == base + i, f32(1.0), jnp.where(block, f32(0.0), row_of(64 + i)))
             for i in range(8)]
        blocks, x = [], {}
        for i in range(0, 8, 2):
            a, b, d = m[i, i], m[i, i + 1], m[i + 1, i + 1]
            det = reciprocal(a * d - b * b)
            v0, v1, v2 = d * det, -b * det, a * det
            blocks.append((v0, v1, v2))
            for j in range(i + 2, 8):
                x[i, j] = v0 * m[i, j] + v1 * m[i + 1, j]
                x[i + 1, j] = v1 * m[i, j] + v2 * m[i + 1, j]
            for j in range(i + 2, 8):
                for h in range(i + 2, j + 1):
                    m[h, j] = m[h, j] - (m[i, h] * x[i, j] + m[i + 1, h] * x[i + 1, j])
            for j in range(i + 2, 8):
                r[j] = r[j] - (x[i, j] * r[i] + x[i + 1, j] * r[i + 1])
        new = [None] * 8
        for i in (6, 4, 2, 0):
            v0, v1, v2 = blocks[i // 2]
            top = v0 * r[i] + v1 * r[i + 1]
            low = v1 * r[i] + v2 * r[i + 1]
            for j in range(i + 2, 8):
                top = top - x[i, j] * new[j]
                low = low - x[i + 1, j] * new[j]
            new[i], new[i + 1] = top, low
        for q in [(p + 1 + z) % count for z in range(count)]:
            target = panels[q]
            if q == p:
                out = new[0]
                for i in range(1, 8):
                    out = jnp.where(row == i, new[i], out)
            else:
                out = jnp.where(block, f32(0.0), target)
                out = out - sum(spread(target, base + j) * new[j] for j in range(8))
            panels[q] = out
    return jnp.concatenate(panels, axis=0)


def modes_kernel(groups, chunks, where_ref, mine_ref, other_ref, *rest):
    blocks = rest[:groups * chunks]
    outs = rest[groups * chunks:groups * (chunks + 1)]
    coupling_ref, stage, held = rest[groups * (chunks + 1):]
    me, half = where_ref[0], where_ref[1]
    mid = mine_ref.shape[0]
    snaps = 2 * mid
    parts = blocks[0].shape[0]
    coupling_ref[pl.ds(pl.multiple_of(half * mid, mid), mid), :] = mine_ref[...]
    coupling_ref[pl.ds(pl.multiple_of((1 - half) * mid, mid), mid), :] = other_ref[...]
    coupled = coupling_ref[...]
    gram = lax.dot_general(coupled, coupled, (((1,), (1,)), ((), ())),
                           precision=lax.Precision.HIGHEST, preferred_element_type=f32)
    r = lax.broadcasted_iota(jnp.int32, (snaps, snaps), 0)
    c = lax.broadcasted_iota(jnp.int32, (snaps, snaps), 1)
    diagonal = jnp.where(r == c, gram, 0.0)
    energy = jnp.sum(jnp.sum(diagonal, axis=0, keepdims=True), axis=1, keepdims=True) / snaps
    system = gram / energy + jnp.where(r == c, f32(damping), f32(0.0))
    inverse = invert(system, held)
    weights = jnp.dot(inverse, coupled, precision=lax.Precision.HIGHEST,
                      preferred_element_type=f32) / jnp.sqrt(energy)
    weights = weights.astype(bf16)
    inverse = inverse.astype(bf16)
    share = snaps // groups
    ny = outs[0].shape[3]
    layers = parts // ny

    def action(mine):
        def group(g, at):
            return [block[at] for block in blocks[peer(mine, g) * chunks:(peer(mine, g) + 1) * chunks]]

        for layer in range(layers):
            for y in range(ny):
                at = layer * ny + y
                rows = pl.ds(y, snaps, stride=ny)
                direct = jnp.concatenate(
                    [part for g in range(groups - 1) for part in group(g, at)], axis=0)
                adjoint = jnp.concatenate(group(groups - 1, at), axis=0)
                stage[0, layer, rows, :] = jnp.dot(weights, direct, preferred_element_type=f32)
                stage[1, layer, rows, :] = jnp.dot(inverse, adjoint, preferred_element_type=f32)

    by_group(me, groups, action)
    for k in range(groups):
        start = pl.multiple_of(peer(me, k) * (share * ny), share * ny)
        for which in range(2):
            for layer in range(layers):
                value = stage[which, layer, pl.ds(start, share * ny), :]
                outs[k][which, :, layer] = value.reshape(share, ny, value.shape[1]).astype(bf16)


def modes(where, mine, other, blocks, groups, ny):
    chunks = len(blocks) // groups
    parts, _, nz = blocks[0].shape
    snaps = 2 * mine.shape[0]
    layers = parts // ny
    share = snaps // groups
    return pl.pallas_call(
        functools.partial(modes_kernel, groups, chunks),
        out_shape=[jax.ShapeDtypeStruct((2, share, layers, ny, nz), bf16)] * groups,
        in_specs=[smem, vmem, vmem] + [vmem] * len(blocks),
        out_specs=[vmem] * groups,
        scratch_shapes=[pltpu.VMEM((snaps, mine.shape[1]), f32),
                        pltpu.VMEM((2, layers, snaps * ny, nz), f32),
                        pltpu.VMEM((2, 72, snaps), f32)],
        compiler_params=pltpu.CompilerParams(vmem_limit_bytes=VMEM_LIMIT),
        name="modes",
    )(where, mine, other, *blocks)


def place_kernel(groups, where_ref, *rest):
    blocks = rest[:groups]
    outs = rest[groups:]
    me = where_ref[0]
    layers = blocks[0].shape[2]
    for k in range(groups):
        for which in range(2):
            for layer in range(layers):
                outs[which][:, peer(me, k) * layers + layer] = blocks[k][which, :, layer]


def place(where, blocks, groups):
    _, share, layers, ny, nz = blocks[0].shape
    out = jax.ShapeDtypeStruct((share, layers * groups, ny, nz), bf16)
    return pl.pallas_call(
        functools.partial(place_kernel, groups),
        out_shape=[out, out],
        in_specs=[smem] + [vmem] * groups,
        out_specs=[vmem] * 2,
        compiler_params=pltpu.CompilerParams(vmem_limit_bytes=8 * 1024 * 1024),
        name="place",
    )(where, *blocks)


def per_device(snapshots, base_flow):
    field = snapshots[0]
    snaps, rows, ny, nz = field.shape
    groups = lax.axis_size("grp")
    slabs = lax.axis_size("slab")
    me = lax.axis_index("grp")
    half = lax.axis_index("slab") % 2
    where = jnp.stack([me, half]).astype(jnp.int32)
    flow = 0.5 * base_flow
    at = jnp.arange(nz)
    gap = (at[:, None] - at[None, :]) % nz
    ring = (2 * (gap == 0) + (gap == 1) + (gap == nz - 1)).astype(bf16)
    sizes = [snaps * part // sum(CHUNKS) for part in CHUNKS]
    chunks = len(sizes)
    blocks = [[None] * chunks for _ in range(groups)]
    coefs = None
    for c in range(chunks):
        own = pack(flow, field, sum(sizes[:c]), sizes[c], c == 0, [inner] if c else [])
        inner = swap(own, "slab", 1)
        outer = swap_outer(own, "slab")
        before = [blocks[1][c - 1]] if c else []
        parts, made = sections(where, ring, coefs, own, inner, outer, groups, flow, before)
        coefs = coefs or made
        blocks[0][c] = parts[0]
        for k in range(1, groups):
            blocks[k][c] = swap(parts[k], "grp", k)
    flat = [blocks[k][c] for k in range(groups) for c in range(chunks)]
    keep, send = coupling(where, flat, groups, chunks)
    total = keep + swap(send, "slab", 1)
    bit = 2
    while bit < slabs:
        steps = [bit]
        if 2 * bit < slabs:
            steps += [2 * bit, 3 * bit]
        sent = total.astype(bf16)
        total = sum((swap(sent, "slab", s).astype(f32) for s in steps), total)
        bit *= 4
    sent = total.astype(bf16)
    total = sum((swap(sent, "grp", s).astype(f32) for s in range(1, groups)), total)
    mine = total * (1.0 / math.sqrt(rows * slabs * ny * nz))
    other = swap(mine, "slab", 1)
    outs = modes(where, mine, other, flat, groups, ny)
    outs = list(outs)
    for k in range(1, groups):
        outs[k] = swap(outs[k], "grp", k)
    return tuple(place(where, outs, groups))


def solution(mesh):
    return jax.shard_map(
        per_device,
        mesh=mesh,
        in_specs=(P("grp", None, "slab", None, None), P("slab", None, None)),
        out_specs=(P("grp", "slab", None, None), P("grp", "slab", None, None)),
        check_vma=False,
    )
```

```python
import functools
import math

import jax
import jax.numpy as jnp
from jax import lax
from jax.experimental import pallas as pl
from jax.experimental.pallas import tpu as pltpu
from jax.sharding import PartitionSpec as P

SECTIONS = 4
CHUNKS = (1, 1)
TALL = 64
TERMS = 2

diffuse_x = 0.35
diffuse_side = 0.05
damping = 0.5

VMEM_LIMIT = 48 * 1024 * 1024
vmem = pl.BlockSpec(memory_space=pltpu.VMEM)
smem = pl.BlockSpec(memory_space=pltpu.SMEM)
anywhere = pl.BlockSpec(memory_space=pl.ANY)
hbm = pl.BlockSpec(memory_space=pltpu.HBM)
f32 = jnp.float32
bf16 = jnp.bfloat16


def peer(index, step):
    return index ^ step


def swap(value, axis, step):
    count = lax.axis_size(axis)
    return lax.ppermute(value, axis, [(i, i ^ step) for i in range(count)])


def swap_outer(value, axis):
    count = lax.axis_size(axis)
    return lax.ppermute(value, axis, [(i, (i + 2 * (i % 2) - 1) % count) for i in range(count)])


def pack_kernel(start, with_flow, flow_ref, field_ref, *rest):
    out, block, stage, flow, sem, flow_sem = rest[-6:]
    step, rows, ny, nz = block.shape
    copy = pltpu.make_async_copy(field_ref.at[pl.ds(start, step)], block, sem)
    copy.start()
    if with_flow:
        flow_copy = pltpu.make_async_copy(flow_ref, flow, flow_sem)
        flow_copy.start()
    copy.wait()
    for r in range(rows):
        stage[r % 2] = block[:, r].astype(f32).reshape(step * ny, nz)
        for y in range(ny):
            out[r * ny + y] = stage[r % 2, pl.ds(y, step, stride=ny), :].astype(bf16)
    if with_flow:
        flow_copy.wait()
        per = step // (rows * ny)
        left = 0.5 * flow[...].reshape(rows * ny, nz)
        for p in range(TERMS):
            part = left.astype(bf16)
            left = left - part.astype(f32)
            at = p % per * rows * ny
            out[rows * ny + p // per, at:at + rows * ny] = part


def pack(flow, field, start, step, with_flow, before):
    _, rows, ny, nz = field.shape
    extra = -(-TERMS // (step // (rows * ny))) if with_flow else 0
    return pl.pallas_call(
        functools.partial(pack_kernel, start, with_flow),
        out_shape=jax.ShapeDtypeStruct((rows * ny + extra, step, nz), bf16),
        in_specs=[hbm, hbm] + [anywhere] * len(before),
        out_specs=vmem,
        scratch_shapes=[
            pltpu.VMEM((step, rows, ny, nz), bf16),
            pltpu.VMEM((2, step * ny, nz), f32),
            pltpu.VMEM((rows, ny, nz), f32),
            pltpu.SemaphoreType.DMA(()),
            pltpu.SemaphoreType.DMA(()),
        ],
        compiler_params=pltpu.CompilerParams(vmem_limit_bytes=VMEM_LIMIT),
        name="pack",
    )(flow, field, *before)


def sections_kernel(groups, rows, ny, lead, where_ref, ring_ref, *rest):
    reach = SECTIONS
    total_rows = rows + 2 * reach
    me = where_ref[0]
    low_core = where_ref[1] == 0
    if lead:
        flow_ref, own_ref, inner_ref, outer_ref = rest[:4]
        outs = rest[4:4 + groups]
        plus, minus, flow_ext, done = rest[4 + groups:]
    else:
        plus, minus, own_ref, inner_ref, outer_ref, _ = rest[:6]
        outs = rest[6:6 + groups]
        done, = rest[6 + groups:]
    step, nz = own_ref.shape[1:]
    if lead:
        adj = (me == groups - 1).astype(jnp.int32)
        sign = jnp.where(me == groups - 1, f32(1.0), f32(-1.0))
        per = step // (rows * ny)

        def flow_of(ref):
            flow = None
            for p in reversed(range(TERMS)):
                at = p % per * rows * ny
                part = ref[rows * ny + p // per, at:at + rows * ny].astype(f32)
                flow = part if flow is None else flow + part
            return flow.reshape(rows, ny, nz)

        inner, outer = flow_of(inner_ref), flow_of(outer_ref)
        flow_ext[0:reach] = jnp.where(low_core, outer, inner)[rows - reach:]
        flow_ext[reach:reach + rows] = flow_ref[...]
        flow_ext[reach + rows:] = jnp.where(low_core, inner, outer)[:reach]
        for e in range(1, total_rows - 1):
            plus[e] = diffuse_x + sign * flow_ext[e + adj]
            minus[e] = diffuse_x - sign * flow_ext[e - adj]
    ring = ring_ref[...]

    def entry(e, y, at):
        if e < reach:
            row = (rows - reach + e) * ny + y
            return jnp.where(low_core, outer_ref[row, at, :], inner_ref[row, at, :])
        if e < reach + rows:
            return own_ref[(e - reach) * ny + y, at, :]
        row = (e - reach - rows) * ny + y
        return jnp.where(low_core, inner_ref[row, at, :], outer_ref[row, at, :])

    tall = math.gcd(step, TALL)

    def body(block, carry):
        at = pl.ds(pl.multiple_of(block * tall, tall), tall)

        def load(e):
            low = [entry(e, y, at) for y in range(ny)]
            return low, [part.astype(f32) for part in low]

        def advance(e, behind, here, ahead):
            low, mid = here
            side = jnp.dot(jnp.concatenate(low, axis=0), ring, preferred_element_type=f32)
            made = []
            for y in range(ny):
                total = side[y * tall:(y + 1) * tall] + (mid[(y + 1) % ny] + mid[(y - 1) % ny])
                total = diffuse_side * total + plus[e, y:y + 1, :] * ahead[1][y]
                total = total + minus[e, y:y + 1, :] * behind[1][y]
                made.append(total.astype(bf16))
            return made, [part.astype(f32) for part in made]

        held = [{} for _ in range(SECTIONS + 1)]
        for t in range(total_rows):
            held[0][t] = load(t)
            for s in range(1, SECTIONS + 1):
                e = t - s
                if s <= e < total_rows - s:
                    below = held[s - 1]
                    held[s][e] = advance(e, below[e - 1], below[e], below[e + 1])
                    del below[e - 1]
                    if s == SECTIONS:
                        for y in range(ny):
                            done[e - reach, y, at, :] = held[s][e][0][y]
        return carry

    lax.fori_loop(0, step // tall, body, 0)
    share = rows // groups
    for k in range(groups):
        for j in range(share):
            outs[k][j * ny:(j + 1) * ny] = done[peer(me, k) * share + j]


def sections(where, ring, coefs, own, inner, outer, groups, flow, before):
    rows, ny, nz = flow.shape
    step = own.shape[1]
    share = rows // groups
    total = rows + 2 * SECTIONS
    lead = coefs is None
    out = [jax.ShapeDtypeStruct((share * ny, step, nz), bf16)] * groups
    scratch = [pltpu.VMEM((rows, ny, step, nz), bf16)]
    if lead:
        out += [jax.ShapeDtypeStruct((total, ny, nz), f32)] * 2
        scratch = [pltpu.VMEM((total, ny, nz), f32)] + scratch
        coefs = [flow]
    outs = pl.pallas_call(
        functools.partial(sections_kernel, groups, rows, ny, lead),
        out_shape=out,
        in_specs=[smem] + [vmem] * (4 + len(coefs)) + [anywhere] * len(before),
        out_specs=[vmem] * len(out),
        scratch_shapes=scratch,
        compiler_params=pltpu.CompilerParams(vmem_limit_bytes=VMEM_LIMIT),
        cost_estimate=pl.CostEstimate(
            flops=8 * SECTIONS * step * total * ny * nz, bytes_accessed=8 * step * rows * ny * nz, transcendentals=0),
        name="sections",
    )(where, ring, *coefs, own, inner, outer, *before)
    return outs[:groups], outs[groups:]


def by_group(me, groups, action):
    for g in range(groups):
        pl.when(me == g)(functools.partial(action, g))


def coupling_kernel(groups, chunks, where_ref, *rest):
    blocks = rest[: groups * chunks]
    keep, send, scratch = rest[groups * chunks:]
    me, half = where_ref[0], where_ref[1]
    parts = blocks[0].shape[0]
    width = 2 if parts % 2 == 0 else 1
    snaps = scratch.shape[0]

    def action(mine):
        def wide(g, y):
            own = blocks[peer(mine, g) * chunks:(peer(mine, g) + 1) * chunks]
            return jnp.concatenate([
                jnp.concatenate([block[y + i] for block in own], axis=0) for i in range(width)
            ], axis=1)

        total = None
        for y in range(0, parts, width):
            direct = jnp.concatenate([wide(g, y) for g in range(groups - 1)], axis=0)
            term = lax.dot_general(wide(groups - 1, y), direct, (((1,), (1,)), ((), ())),
                                   preferred_element_type=f32)
            total = term if total is None else total + term
        scratch[...] = total

    by_group(me, groups, action)
    mid = snaps // 2
    keep[...] = scratch[pl.ds(pl.multiple_of(half * mid, mid), mid), :]
    send[...] = scratch[pl.ds(pl.multiple_of((1 - half) * mid, mid), mid), :]


def coupling(where, blocks, groups, chunks):
    snaps = sum(block.shape[1] for block in blocks[:chunks])
    wide = (groups - 1) * snaps
    return pl.pallas_call(
        functools.partial(coupling_kernel, groups, chunks),
        out_shape=[jax.ShapeDtypeStruct((snaps // 2, wide), f32)] * 2,
        in_specs=[smem] + [vmem] * (groups * chunks),
        out_specs=[vmem] * 2,
        scratch_shapes=[pltpu.VMEM((snaps, wide), f32)],
        compiler_params=pltpu.CompilerParams(vmem_limit_bytes=VMEM_LIMIT),
        name="coupling",
    )(where, *blocks)


def invert(system, held):
    size = system.shape[0]
    count = size // 8
    panels = [system[8 * i:8 * i + 8] for i in range(count)]
    lane = lax.broadcasted_iota(jnp.int32, (8, size), 1)
    row = lax.broadcasted_iota(jnp.int32, (8, size), 0)

    def spread(panel, j):
        return jnp.broadcast_to(panel[:, j:j + 1], (8, size))

    def reciprocal(value):
        guess = pl.reciprocal(value, approx=True)
        guess = guess * (2.0 - value * guess)
        return guess * (2.0 - value * guess)

    for p in range(count):
        base, slot = 8 * p, p % 2
        lead = panels[p]
        for j in range(8):
            held[slot, 8 * j:8 * j + 8, :] = spread(lead, base + j)
        held[slot, 64:72, :] = lead

        def row_of(at, slot=slot):
            return jnp.broadcast_to(held[slot, at:at + 1, :], (8, size))

        m = {(i, j): row_of(8 * j + i) for j in range(8) for i in range(j + 1)}
        block = (lane >= base) & (lane < base + 8)
        r = [jnp.where(lane == base + i, f32(1.0), jnp.where(block, f32(0.0), row_of(64 + i)))
             for i in range(8)]
        blocks, x = [], {}
        for i in range(0, 8, 2):
            a, b, d = m[i, i], m[i, i + 1], m[i + 1, i + 1]
            det = reciprocal(a * d - b * b)
            v0, v1, v2 = d * det, -b * det, a * det
            blocks.append((v0, v1, v2))
            for j in range(i + 2, 8):
                x[i, j] = v0 * m[i, j] + v1 * m[i + 1, j]
                x[i + 1, j] = v1 * m[i, j] + v2 * m[i + 1, j]
            for j in range(i + 2, 8):
                for h in range(i + 2, j + 1):
                    m[h, j] = m[h, j] - (m[i, h] * x[i, j] + m[i + 1, h] * x[i + 1, j])
            for j in range(i + 2, 8):
                r[j] = r[j] - (x[i, j] * r[i] + x[i + 1, j] * r[i + 1])
        new = [None] * 8
        for i in (6, 4, 2, 0):
            v0, v1, v2 = blocks[i // 2]
            top = v0 * r[i] + v1 * r[i + 1]
            low = v1 * r[i] + v2 * r[i + 1]
            for j in range(i + 2, 8):
                top = top - x[i, j] * new[j]
                low = low - x[i + 1, j] * new[j]
            new[i], new[i + 1] = top, low
        for q in [(p + 1 + z) % count for z in range(count)]:
            target = panels[q]
            if q == p:
                out = new[0]
                for i in range(1, 8):
                    out = jnp.where(row == i, new[i], out)
            else:
                out = jnp.where(block, f32(0.0), target)
                out = out - sum(spread(target, base + j) * new[j] for j in range(8))
            panels[q] = out
    return jnp.concatenate(panels, axis=0)


def modes_kernel(groups, chunks, where_ref, mine_ref, other_ref, *rest):
    blocks = rest[:groups * chunks]
    outs = rest[groups * chunks:groups * (chunks + 1)]
    coupling_ref, stage, held = rest[groups * (chunks + 1):]
    me, half = where_ref[0], where_ref[1]
    mid = mine_ref.shape[0]
    snaps = 2 * mid
    parts = blocks[0].shape[0]
    coupling_ref[pl.ds(pl.multiple_of(half * mid, mid), mid), :] = mine_ref[...]
    coupling_ref[pl.ds(pl.multiple_of((1 - half) * mid, mid), mid), :] = other_ref[...]
    coupled = coupling_ref[...]
    gram = lax.dot_general(coupled, coupled, (((1,), (1,)), ((), ())),
                           precision=lax.Precision.HIGHEST, preferred_element_type=f32)
    r = lax.broadcasted_iota(jnp.int32, (snaps, snaps), 0)
    c = lax.broadcasted_iota(jnp.int32, (snaps, snaps), 1)
    diagonal = jnp.where(r == c, gram, 0.0)
    energy = jnp.sum(jnp.sum(diagonal, axis=0, keepdims=True), axis=1, keepdims=True) / snaps
    system = gram / energy + jnp.where(r == c, f32(damping), f32(0.0))
    inverse = invert(system, held)
    weights = jnp.dot(inverse, coupled, precision=lax.Precision.HIGHEST,
                      preferred_element_type=f32) / jnp.sqrt(energy)
    weights = weights.astype(bf16)
    inverse = inverse.astype(bf16)
    share = snaps // groups
    ny = outs[0].shape[3]
    layers = parts // ny

    def action(mine):
        def group(g, at):
            return [block[at] for block in blocks[peer(mine, g) * chunks:(peer(mine, g) + 1) * chunks]]

        for layer in range(layers):
            for y in range(ny):
                at = layer * ny + y
                rows = pl.ds(y, snaps, stride=ny)
                direct = jnp.concatenate(
                    [part for g in range(groups - 1) for part in group(g, at)], axis=0)
                adjoint = jnp.concatenate(group(groups - 1, at), axis=0)
                stage[0, layer, rows, :] = jnp.dot(weights, direct, preferred_element_type=f32)
                stage[1, layer, rows, :] = jnp.dot(inverse, adjoint, preferred_element_type=f32)

    by_group(me, groups, action)
    for k in range(groups):
        start = pl.multiple_of(peer(me, k) * (share * ny), share * ny)
        for which in range(2):
            for layer in range(layers):
                value = stage[which, layer, pl.ds(start, share * ny), :]
                outs[k][which, :, layer] = value.reshape(share, ny, value.shape[1]).astype(bf16)


def modes(where, mine, other, blocks, groups, ny):
    chunks = len(blocks) // groups
    parts, _, nz = blocks[0].shape
    snaps = 2 * mine.shape[0]
    layers = parts // ny
    share = snaps // groups
    return pl.pallas_call(
        functools.partial(modes_kernel, groups, chunks),
        out_shape=[jax.ShapeDtypeStruct((2, share, layers, ny, nz), bf16)] * groups,
        in_specs=[smem, vmem, vmem] + [vmem] * len(blocks),
        out_specs=[vmem] * groups,
        scratch_shapes=[pltpu.VMEM((snaps, mine.shape[1]), f32),
                        pltpu.VMEM((2, layers, snaps * ny, nz), f32),
                        pltpu.VMEM((2, 72, snaps), f32)],
        compiler_params=pltpu.CompilerParams(vmem_limit_bytes=VMEM_LIMIT),
        name="modes",
    )(where, mine, other, *blocks)


def place_kernel(groups, where_ref, *rest):
    blocks = rest[:groups]
    outs = rest[groups:]
    me = where_ref[0]
    layers = blocks[0].shape[2]
    for k in range(groups):
        for which in range(2):
            for layer in range(layers):
                outs[which][:, peer(me, k) * layers + layer] = blocks[k][which, :, layer]


def place(where, blocks, groups):
    _, share, layers, ny, nz = blocks[0].shape
    out = jax.ShapeDtypeStruct((share, layers * groups, ny, nz), bf16)
    return pl.pallas_call(
        functools.partial(place_kernel, groups),
        out_shape=[out, out],
        in_specs=[smem] + [vmem] * groups,
        out_specs=[vmem] * 2,
        compiler_params=pltpu.CompilerParams(vmem_limit_bytes=8 * 1024 * 1024),
        name="place",
    )(where, *blocks)


def per_device(snapshots, base_flow):
    field = snapshots[0]
    snaps, rows, ny, nz = field.shape
    groups = lax.axis_size("grp")
    slabs = lax.axis_size("slab")
    me = lax.axis_index("grp")
    half = lax.axis_index("slab") % 2
    where = jnp.stack([me, half]).astype(jnp.int32)
    flow = 0.5 * base_flow
    at = jnp.arange(nz)
    gap = (at[:, None] - at[None, :]) % nz
    ring = (2 * (gap == 0) + (gap == 1) + (gap == nz - 1)).astype(bf16)
    sizes = [snaps * part // sum(CHUNKS) for part in CHUNKS]
    chunks = len(sizes)
    blocks = [[None] * chunks for _ in range(groups)]
    coefs = None
    for c in range(chunks):
        own = pack(base_flow, field, sum(sizes[:c]), sizes[c], c == 0, [inner] if c else [])
        inner = swap(own, "slab", 1)
        outer = swap_outer(own, "slab")
        before = [blocks[1][c - 1]] if c else []
        parts, made = sections(where, ring, coefs, own, inner, outer, groups, flow, before)
        coefs = coefs or made
        blocks[0][c] = parts[0]
        for k in range(1, groups):
            blocks[k][c] = swap(parts[k], "grp", k)
    flat = [blocks[k][c] for k in range(groups) for c in range(chunks)]
    keep, send = coupling(where, flat, groups, chunks)
    total = keep + swap(send.astype(bf16), "slab", 1).astype(f32)
    bit = 2
    while bit < slabs:
        steps = [bit]
        if 2 * bit < slabs:
            steps += [2 * bit, 3 * bit]
        sent = total.astype(bf16)
        total = sum((swap(sent, "slab", s).astype(f32) for s in steps), total)
        bit *= 4
    sent = total.astype(bf16)
    total = sum((swap(sent, "grp", s).astype(f32) for s in range(1, groups)), total)
    mine = total * (1.0 / math.sqrt(rows * slabs * ny * nz))
    other = swap(mine, "slab", 1)
    outs = modes(where, mine, other, flat, groups, ny)
    outs = list(outs)
    for k in range(1, groups):
        outs[k] = swap(outs[k], "grp", k)
    return tuple(place(where, outs, groups))


def solution(mesh):
    return jax.shard_map(
        per_device,
        mesh=mesh,
        in_specs=(P("grp", None, "slab", None, None), P("slab", None, None)),
        out_specs=(P("grp", "slab", None, None), P("grp", "slab", None, None)),
        check_vma=False,
    )
```
